32 devices in a mesh: groups: 2 (over y), render: 8 (over z, x), view: 2 (over core).
Axes of the slice: x: 2, y: 2, z: 4, core: 2. Of those that a mesh axis runs over, the one named last changes fastest.
Arguments:
- gaussians: bfloat16 [59, 65536], P(None, ('groups', 'render')), parts along dimension 1, as said below
- camera: float32 [4, 8], P(('groups', 'view')), parts along dimension 0, may hold values from -16 to 16
- eye_point: float32 [4, 3], P(('groups', 'view')), parts along dimension 0, may hold values from 3 to 5
- send_lists: int32 [4, 8, 8, 2], P(('groups', 'view'), 'render'), parts along dimension 0, may hold values from 0 to 32, as said below
- tile_lists: int32 [4, 128, 256], P(('groups', 'view'), 'render'), parts along dimension 0, may hold values from 0 to 2047, as said below
- moving_blocks: int32 [64], P('groups'), parts along dimension 0, may hold values from 0 to 1, as said below
- image_grad: float32 [4, 3, 128, 256], P(('groups', 'view'), None, 'render'), parts along dimension 0, may hold values from -6 to 6
Outputs:
- rendered: float32 [4, 3, 128, 256], P(('groups', 'view'), None, 'render'), parts along dimension 0
- gradients: float32 [59, 65536], P(None, ('groups', 'render')), parts along dimension 1
The draws below stay inside these ranges and needn't reach their ends.
There are 2 independent parts, one for each index of `groups`. The reference program is written for one: setup_inputs(seed, part) draws one part's arguments, and reference() takes and returns one part's arrays. A program takes and returns all parts, laid end to end along the dimension named above; each array names one. Nothing has to cross between parts.
Inputs may be any that keep to these rules, and one draw needn't show every extreme that they name: `gaussians`: row 6 of every column lies between 1 and 2 and rows 7 to 9 between -0.9 and 0.9. `send_lists`: A value 32 marks an empty slot; the blocks of one view, owner and renderer are distinct. In each view every renderer receives 2 or more live blocks in all, and some renderer receives all 2 slots live from every owner. `tile_lists`: the entries of one tile are distinct and name live slots (send_lists below 32) of the tile's renderer, t // 16, in that view. `moving_blocks`: at least one block position moves.
All inputs are finite; a program needn't handle non-finite values.
Results may differ from the reference program's by a relative error of at most 0.0003.
Values may be sent and summed in bfloat16 or wider, within the bound.
A program may use at most 128 MiB of HBM per device.

```python
import math
import jax
import jax.numpy as jnp
from jax import lax

PAR = 59
BLK = 128
LBLK = 2
LIST = 256
TSIDE = 16
PIX = 256
TILE_DEV = 16
TILES = 128
NBLK = 32
CAP = 2
N_RENDER = 8
N_VIEW = 2


def live_slots(key):
    key = jax.random.fold_in(key, 101)
    keys = jax.random.split(key, 4)
    shape = (N_VIEW, N_RENDER, N_RENDER, CAP)
    rate_level = jax.random.randint(keys[0], (N_VIEW, 1, N_RENDER, 1), 1, 11)
    throws = jax.random.randint(keys[1], shape, 0, 10)
    full_dest = jax.random.randint(keys[2], (N_VIEW, 1, 1, 1), 0, N_RENDER)
    source = lax.broadcasted_iota(jnp.int32, shape, 1)
    dest_idx = lax.broadcasted_iota(jnp.int32, shape, 2)
    slot_idx = lax.broadcasted_iota(jnp.int32, shape, 3)
    ahead = (source - dest_idx) % N_RENDER
    is_live = (throws < rate_level) | (dest_idx == full_dest) | (ahead < LBLK) & (slot_idx == 0)
    first_block = jax.random.randint(keys[3], (N_VIEW, N_RENDER, N_RENDER, 1), 0, NBLK)
    block_idx = (first_block + slot_idx) % NBLK
    return jnp.where(is_live, block_idx, NBLK).astype(jnp.int32)


def draw_send_lists(key, part):
    return live_slots(key)


def draw_tile_lists(key, part):
    slots = live_slots(key)
    key = jax.random.fold_in(key, 7)
    receive = N_RENDER * CAP * BLK
    tile_keys = jax.random.split(key, N_VIEW * TILES)
    views = jnp.repeat(jnp.arange(N_VIEW, dtype=jnp.int32), TILES)
    tiles = jnp.tile(jnp.arange(TILES, dtype=jnp.int32), N_VIEW)

    def one_tile(items):
        tile_key, view, tile = items
        renderer = tile // TILE_DEV
        column = lax.dynamic_index_in_dim(lax.dynamic_index_in_dim(slots, view, 0, False), renderer, 1, False)
        is_live = (column < NBLK).astype(jnp.int32).reshape(-1)
        live_entry = jnp.repeat(is_live, BLK)
        order = jax.random.permutation(tile_key, receive).astype(jnp.int32)
        scores = live_entry * receive + order
        return lax.top_k(scores, LIST)[1].astype(jnp.int32)
    chosen = lax.map(one_tile, (tile_keys, views, tiles))
    return chosen.reshape(N_VIEW, TILES, LIST)


def draw_moving_blocks(key, part):
    key = jax.random.fold_in(key, 13)
    keys = jax.random.split(key, 2)
    flags = (jax.random.randint(keys[0], (NBLK,), 0, 4) == 0).astype(jnp.int32)
    forced = jax.random.randint(keys[1], (), 0, NBLK)
    return jnp.where(jnp.arange(NBLK, dtype=jnp.int32) == forced, 1, flags).astype(jnp.int32)


def draw_gaussians(key, part):
    key = jax.random.fold_in(key, 29)
    keys = jax.random.split(key, 8)
    count = NBLK * BLK * N_RENDER
    degree_zero = (jnp.arange(48) % 16 == 0)[:, None]
    base_colour = jax.random.uniform(keys[7], (48, count), jnp.float32, -3.0, 30.0)
    opacity_logit = jax.random.uniform(keys[4], (1, count), jnp.float32, -10.0, -6.0)
    position = jax.random.uniform(keys[0], (3, count), jnp.float32, -1.0, 1.0)
    log_scale = jax.random.uniform(keys[1], (3, count), jnp.float32, math.log(0.2), math.log(0.8))
    leading = jax.random.uniform(keys[2], (1, count), jnp.float32, 1.0, 2.0)
    trailing = jnp.clip(0.4 * jax.random.normal(keys[3], (3, count), jnp.float32), -0.9, 0.9)
    varying = 2.0 * jax.random.normal(keys[6], (48, count), jnp.float32)
    harmonic = jnp.where(degree_zero, base_colour, varying)
    whole = jnp.concatenate([position, log_scale, leading, trailing, opacity_logit, harmonic], axis=0)
    return whole.astype(jnp.bfloat16)


def block_levels(own_key, dims, pieces, least, high):
    loudness = 1.0
    for dim, shards_of in pieces:
        steps = jax.random.uniform(jax.random.fold_in(jax.random.fold_in(own_key, 6), dim), (shards_of,), jnp.float32, least / len(pieces), high / len(pieces))
        loudness = loudness * jnp.repeat(jnp.exp(steps), dims[dim] // shards_of).reshape((-1,) + (1,) * (len(dims) - 1 - dim))
    return loudness


def bell_draw(own_key, shape, width, bound, cuts=(), held_as=jnp.bfloat16):
    values = jax.random.normal(own_key, shape, jnp.float32) * width
    if len(cuts) > 0:
        values = block_levels(own_key, shape, cuts, -0.22, 0.18) * values
    return jnp.clip(values, min=-bound, max=bound).astype(held_as)


def setup_inputs(seed: int = 0, part: int = 0) -> dict:
    key_of = jax.random.split(jax.random.key(seed), 8)
    own_keys = jax.random.split(jax.random.fold_in(key_of[7], part), 8)
    gaussians = draw_gaussians(jax.random.fold_in(jax.random.fold_in(key_of[7], part), 71), part)
    camera = bell_draw(own_keys[1], (N_VIEW, 8), 4.0, 16.0, ((0, 2),), jnp.float32)
    eye_point = jnp.clip(3.0 + 2.0 * jax.random.uniform(own_keys[2], (N_VIEW, 3), jnp.float32) ** block_levels(own_keys[2], (N_VIEW, 3), ((0, 2),), -0.2, 0.2), 3.0, 5.0)
    send_lists = draw_send_lists(jax.random.fold_in(jax.random.fold_in(key_of[7], part), 71), part)
    tile_lists = draw_tile_lists(jax.random.fold_in(jax.random.fold_in(key_of[7], part), 71), part)
    moving_blocks = draw_moving_blocks(jax.random.fold_in(jax.random.fold_in(key_of[7], part), 71), part)
    image_grad = bell_draw(own_keys[6], (N_VIEW, 3, TILES, PIX), 1.0, 6.0, ((0, 2), (2, 8)), jnp.float32)
    return dict(gaussians=gaussians, camera=camera, eye_point=eye_point, send_lists=send_lists, tile_lists=tile_lists, moving_blocks=moving_blocks, image_grad=image_grad)


LOW_PASS = 0.3
SH_ZERO = 0.28209479177387814
SH_ONE = 0.4886025119029199
SH_TWO = (1.0925484305920792, -1.0925484305920792, 0.31539156525252005, -1.0925484305920792, 0.5462742152960396)
SH_THREE = (-0.5900435899266435, 2.890611442640554, -0.4570457994644658, 0.3731763325901154, -0.4570457994644658, 1.445305721320277, -0.5900435899266435)

def harmonics(x, y, z):
    xx, yy, zz = (x * x, y * y, z * z)
    return [SH_ZERO * jnp.ones_like(x), -SH_ONE * y, SH_ONE * z, -SH_ONE * x, SH_TWO[0] * x * y, SH_TWO[1] * y * z, SH_TWO[2] * (2.0 * zz - xx - yy), SH_TWO[3] * x * z, SH_TWO[4] * (xx - yy), SH_THREE[0] * y * (3.0 * xx - yy), SH_THREE[1] * x * y * z, SH_THREE[2] * y * (4.0 * zz - xx - yy), SH_THREE[3] * z * (2.0 * zz - 3.0 * xx - 3.0 * yy), SH_THREE[4] * x * (4.0 * zz - xx - yy), SH_THREE[5] * z * (xx - yy), SH_THREE[6] * x * (xx - 3.0 * yy)]

def project(parameters, camera_row, eye_row):
    position = parameters[0:3]
    variance = jnp.exp(2.0 * parameters[3:6])
    quaternion = parameters[6:10]
    quat_norm = jnp.sqrt(lax.optimization_barrier(jnp.sum(quaternion * quaternion, axis=0)))
    unit = quaternion / quat_norm
    w, x, y, z = (unit[0], unit[1], unit[2], unit[3])
    rotation = [[1.0 - 2.0 * (y * y + z * z), 2.0 * (x * y - w * z), 2.0 * (x * z + w * y)], [2.0 * (x * y + w * z), 1.0 - 2.0 * (x * x + z * z), 2.0 * (y * z - w * x)], [2.0 * (x * z - w * y), 2.0 * (y * z + w * x), 1.0 - 2.0 * (x * x + y * y)]]
    mapped = [[sum((camera_row[3 * a + i] * rotation[i][k] for i in range(3))) for k in range(3)] for a in range(2)]
    cov_xx = sum((mapped[0][k] * mapped[0][k] * variance[k] for k in range(3))) + LOW_PASS
    cov_xy = sum((mapped[0][k] * mapped[1][k] * variance[k] for k in range(3)))
    cov_yy = sum((mapped[1][k] * mapped[1][k] * variance[k] for k in range(3))) + LOW_PASS
    determinant = cov_xx * cov_yy - cov_xy * cov_xy
    mean_x = sum((camera_row[i] * position[i] for i in range(3))) + camera_row[6]
    mean_y = sum((camera_row[3 + i] * position[i] for i in range(3))) + camera_row[7]
    opacity = jax.nn.sigmoid(parameters[10])
    direction = position - eye_row[:, None]
    distance = jnp.sqrt(lax.optimization_barrier(jnp.sum(direction * direction, axis=0)))
    basis = harmonics(direction[0] / distance, direction[1] / distance, direction[2] / distance)
    colours = []
    for channel in range(3):
        total = sum((basis[k] * parameters[11 + 16 * channel + k] for k in range(16)))
        colours.append(jnp.maximum(total + 0.5, 0.0))
    return jnp.stack([mean_x, mean_y, cov_yy / determinant, -cov_xy / determinant, cov_xx / determinant, opacity] + colours)

def pixel_grid():
    side = jnp.arange(TSIDE, dtype=jnp.float32) - (TSIDE - 1) / 2.0
    return (jnp.tile(side, TSIDE), jnp.repeat(side, TSIDE))

def shade(records, pixel_x, pixel_y):
    delta_x = pixel_x[:, None] - records[0][None, :]
    delta_y = pixel_y[:, None] - records[1][None, :]
    power = -0.5 * (records[2][None, :] * delta_x * delta_x + records[4][None, :] * delta_y * delta_y) - records[3][None, :] * delta_x * delta_y
    alpha = records[5][None, :] * jnp.exp(power)
    return (alpha, jnp.log1p(-alpha))

def blend(records, pixel_x, pixel_y):
    alpha, keeping = shade(records, pixel_x, pixel_y)
    total = jnp.cumsum(keeping, axis=1)
    before = jnp.concatenate([jnp.zeros((keeping.shape[0], 1), keeping.dtype), total[:, :-1]], axis=1)
    weight = alpha * jnp.exp(before)
    return jnp.einsum('cl,pl->cp', records[6:9], weight, precision=lax.Precision.HIGHEST)

def reference(gaussians, camera, eye_point, send_lists, tile_lists, moving_blocks, image_grad):
    params = gaussians.astype(jnp.float32)
    pixel_x, pixel_y = pixel_grid()
    tiles = jnp.arange(TILES, dtype=jnp.int32)

    def images_of(parameters):
        pictures = []
        for view in range(N_VIEW):
            records = project(parameters, camera[view], eye_point[view])
            entries = tile_lists[view]
            source = entries // (CAP * BLK)
            slot_idx = entries // BLK % CAP
            offset = entries % BLK
            renderer = jnp.broadcast_to((tiles // TILE_DEV)[:, None], entries.shape)
            block_idx = send_lists[view][source, renderer, slot_idx]
            gauss_ids = (source * (NBLK * BLK) + block_idx * BLK + offset).astype(jnp.int32)
            picked = jnp.take(records, gauss_ids.reshape(-1), axis=1).reshape(records.shape[0], TILES, LIST)

            def one_tile(tile_records):
                return blend(tile_records, pixel_x, pixel_y)
            picture = lax.map(jax.checkpoint(one_tile), jnp.moveaxis(picked, 1, 0))
            pictures.append(jnp.moveaxis(picture, 0, 1))
        return jnp.stack(pictures)
    rendered, pullback = jax.vjp(images_of, params)
    raw_grads = pullback(image_grad.astype(jnp.float32))[0]
    blocks = raw_grads.reshape(PAR, N_RENDER, NBLK, BLK)
    rolled = jnp.roll(blocks, 1, axis=1)
    moves = (moving_blocks == 1)[None, None, :, None]
    gradients = jnp.where(moves, rolled, blocks).reshape(PAR, N_RENDER * NBLK * BLK)
    return (rendered, gradients)
```

```python
import jax
import jax.numpy as jnp
from jax import lax
from jax.experimental import pallas as pl
from jax.experimental.pallas import tpu as pltpu
from jax.sharding import PartitionSpec as P

PAR = 59
BLK = 128
TSIDE = 16
PIX = TSIDE * TSIDE
NBLK = 32
CAP = 2
ROWS = 16
ID_ROW = 9
CAM_ROW = 10
SEG = 8

LOW_PASS = 0.3
SH_ZERO = 0.28209479177387814
SH_ONE = 0.4886025119029199
SH_TWO = (
    1.0925484305920792,
    -1.0925484305920792,
    0.31539156525252005,
    -1.0925484305920792,
    0.5462742152960396,
)
SH_THREE = (
    -0.5900435899266435,
    2.890611442640554,
    -0.4570457994644658,
    0.3731763325901154,
    -0.4570457994644658,
    1.445305721320277,
    -0.5900435899266435,
)
F32 = jnp.float32
BF16 = jnp.bfloat16


def harmonics(x, y, z):
    xx, yy, zz = (x * x, y * y, z * z)
    return [
        SH_ZERO * jnp.ones_like(x),
        -SH_ONE * y,
        SH_ONE * z,
        -SH_ONE * x,
        SH_TWO[0] * x * y,
        SH_TWO[1] * y * z,
        SH_TWO[2] * (2.0 * zz - xx - yy),
        SH_TWO[3] * x * z,
        SH_TWO[4] * (xx - yy),
        SH_THREE[0] * y * (3.0 * xx - yy),
        SH_THREE[1] * x * y * z,
        SH_THREE[2] * y * (4.0 * zz - xx - yy),
        SH_THREE[3] * z * (2.0 * zz - 3.0 * xx - 3.0 * yy),
        SH_THREE[4] * x * (4.0 * zz - xx - yy),
        SH_THREE[5] * z * (xx - yy),
        SH_THREE[6] * x * (xx - 3.0 * yy),
    ]


def total_of(terms):
    total = terms[0]
    for term in terms[1:]:
        total = total + term
    return total


def shape_coefs(position, scales, quaternion, cam):
    variance = [jnp.exp(2.0 * s) for s in scales]
    inverse = 1.0 / jnp.sqrt(total_of([c * c for c in quaternion]))
    w, x, y, z = [c * inverse for c in quaternion]
    rotation = [
        [1.0 - 2.0 * (y * y + z * z), 2.0 * (x * y - w * z), 2.0 * (x * z + w * y)],
        [2.0 * (x * y + w * z), 1.0 - 2.0 * (x * x + z * z), 2.0 * (y * z - w * x)],
        [2.0 * (x * z - w * y), 2.0 * (y * z + w * x), 1.0 - 2.0 * (x * x + y * y)],
    ]
    mapped = [
        [total_of([cam[3 * a + i] * rotation[i][k] for i in range(3)]) for k in range(3)]
        for a in range(2)
    ]
    scaled = [mapped[0][k] * variance[k] for k in range(3)]
    cov_xx = total_of([scaled[k] * mapped[0][k] for k in range(3)]) + LOW_PASS
    cov_xy = total_of([scaled[k] * mapped[1][k] for k in range(3)])
    cov_yy = total_of([mapped[1][k] * mapped[1][k] * variance[k] for k in range(3)]) + LOW_PASS
    over = 1.0 / (cov_xx * cov_yy - cov_xy * cov_xy)
    conic_a, conic_b, conic_c = (cov_yy * over, -cov_xy * over, cov_xx * over)
    mean_x = total_of([cam[i] * position[i] for i in range(3)]) + cam[6]
    mean_y = total_of([cam[3 + i] * position[i] for i in range(3)]) + cam[7]
    lin_x = conic_a * mean_x + conic_b * mean_y
    lin_y = conic_b * mean_x + conic_c * mean_y
    const = -0.5 * (lin_x * mean_x + lin_y * mean_y)
    return [-0.5 * conic_a, -0.5 * conic_c, -conic_b, lin_x, lin_y, const]


def basis_of(position, eye):
    direction = [position[i] - eye[i] for i in range(3)]
    inverse = 1.0 / jnp.sqrt(total_of([c * c for c in direction]))
    return harmonics(*[c * inverse for c in direction])


def log_sigmoid(x):
    return jnp.minimum(x, 0.0) - jnp.log1p(jnp.exp(-jnp.abs(x)))


def project_kernel(gauss_ref, cam_ref, row_ref, out_ref, par_ref):
    for b in range(NBLK):
        par_ref[pl.ds(b, PAR, stride=NBLK), :] = gauss_ref[:, b * BLK : (b + 1) * BLK].astype(F32)
    cam = [cam_ref[0, i] for i in range(8)]
    eye = [cam_ref[0, 8 + i] for i in range(3)]

    def chunk(c, carry):
        at = pl.multiple_of(c * 8, 8)

        def par(k):
            return par_ref[pl.ds(k * NBLK + at, 8), :]

        position = [par(k) for k in range(3)]
        coefs = shape_coefs(position, [par(3 + k) for k in range(3)], [par(6 + k) for k in range(4)], cam)
        coefs[5] = coefs[5] + log_sigmoid(par(10))
        basis = basis_of(position, eye)
        rows = []
        for ch in range(3):
            colour = total_of([basis[k] * par(11 + 16 * ch + k) for k in range(16)])
            rows.append(jnp.maximum(colour + 0.5, 0.0))
        rows += coefs
        rows.append((lax.broadcasted_iota(jnp.int32, (8, BLK), 0) + at).astype(F32))
        rows.append(jnp.broadcast_to(row_ref[...], (8, BLK)))
        for k in range(ROWS):
            value = rows[k] if k < len(rows) else jnp.zeros((8, BLK), F32)
            out_ref[k, pl.ds(at, 8), :] = value
        return carry

    lax.fori_loop(0, NBLK // 8, chunk, 0)


def split(values, count):
    pieces = []
    rest = values
    for i in range(count):
        piece = rest.astype(BF16)
        pieces.append(piece)
        if i + 1 < count:
            rest = rest - piece.astype(F32)
    return pieces


def dot_tn(a, b):
    return lax.dot_general(a, b, (((0,), (0,)), ((), ())), preferred_element_type=F32)


def dot_nt(a, b):
    return lax.dot_general(a, b, (((1,), (1,)), ((), ())), preferred_element_type=F32)


def dot_nn(a, b):
    return lax.dot_general(a, b, (((1,), (0,)), ((), ())), preferred_element_type=F32)


def render_kernel(rec_ref, list_ref, cot_ref, mono_ref, image_ref, grad_ref):
    slots = rec_ref.shape[0]
    tiles, entries = list_ref.shape
    group = min(slots, 16)
    grad_ref[...] = jnp.zeros_like(grad_ref)
    mono = mono_ref[...]
    mono_three = jnp.concatenate([mono, mono, mono], axis=0)

    def tile(t, carry):
        index = list_ref[pl.ds(t, 1), :]
        lane = jnp.bitwise_and(index, BLK - 1)
        slot = jnp.right_shift(index, 7)
        picked = []
        for start in range(0, entries, BLK):
            lanes = jnp.broadcast_to(lane[:, start : start + BLK], (ROWS, BLK))
            owner = jnp.broadcast_to(slot[:, start : start + BLK], (ROWS, BLK))

            def pick(s, found):
                taken = jnp.take_along_axis(rec_ref[s], lanes, axis=1, mode="promise_in_bounds")
                return jnp.where(owner == s, taken, found)

            found = jnp.zeros((ROWS, BLK), F32)
            if slots <= 16:
                for s in range(slots):
                    found = pick(s, found)
            else:
                found = lax.fori_loop(0, slots, pick, found)
            picked.append(found)
        records = jnp.concatenate(picked, axis=1)
        rec_three = jnp.concatenate(split(records, 3), axis=0)
        cot_one, cot_two = split(cot_ref[t], 2)
        power = dot_tn(rec_three, mono_three)
        toward = dot_tn(
            jnp.concatenate([rec_three, rec_three], axis=0),
            jnp.concatenate([cot_one] * 3 + [cot_two] * 3, axis=0),
        )
        steps = entries // SEG
        keep = jnp.ones((SEG, PIX), F32)
        seen = jnp.zeros((SEG, PIX), F32)
        alphas, weights = ([], [])
        for r in range(steps):
            alpha = jnp.exp(power[r * SEG : (r + 1) * SEG])
            weight = alpha * keep
            seen = seen + weight * toward[r * SEG : (r + 1) * SEG]
            keep = keep - weight
            alphas.append(alpha)
            weights.append(weight)
        front = [jnp.ones((1, PIX), F32)]
        for s in range(SEG - 1):
            front.append(front[-1] * keep[s : s + 1])
        behind = [jnp.zeros((1, PIX), F32)]
        for s in range(SEG - 1, 0, -1):
            behind.append(seen[s : s + 1] + keep[s : s + 1] * behind[-1])
        front = jnp.concatenate(front, axis=0)
        back = jnp.concatenate(behind[::-1], axis=0)
        slopes = [None] * steps
        for r in range(steps - 1, -1, -1):
            weight = weights[r] * front
            weights[r] = weight
            change = toward[r * SEG : (r + 1) * SEG] - back
            slopes[r] = weight * change
            back = back + alphas[r] * change
        weight_one, weight_two = split(jnp.concatenate(weights, axis=0), 2)
        slope_one, slope_two = split(jnp.concatenate(slopes, axis=0), 2)
        image = dot_nn(rec_three, weight_one) + dot_nn(rec_three, weight_two)
        image = image[:ROWS] + image[ROWS : 2 * ROWS] + image[2 * ROWS :]
        for ch in range(3):
            image_ref[ch, pl.ds(t, 1), :] = image[ch : ch + 1]
        cot_both = jnp.concatenate([cot_one, cot_two], axis=0)
        colour_grad = dot_nt(cot_both, weight_one) + dot_nt(cot_both, weight_two)
        shape_grad = dot_nt(mono, slope_one) + dot_nt(mono, slope_two)
        entry_grad = colour_grad[:ROWS] + colour_grad[ROWS:] + shape_grad
        pieces = split(entry_grad, 2)
        where_lane = lax.broadcasted_iota(jnp.int32, (BLK, entries), 0) == lane
        where_lane = where_lane.astype(F32).astype(BF16)

        def spread(first, carry):
            total = None
            masks = [(slot == first + s).astype(F32).astype(BF16) for s in range(group)]
            for piece in pieces:
                stacked = jnp.concatenate([piece * mask for mask in masks], axis=0)
                part = dot_nt(stacked, where_lane)
                total = part if total is None else total + part
            grad_ref[pl.ds(first, group)] += total.reshape(group, ROWS, BLK)
            return carry

        if slots == group:
            spread(0, 0)
        else:
            lax.fori_loop(0, slots // group, lambda i, c: spread(i * group, c), 0)
        return carry

    lax.fori_loop(0, tiles, tile, 0)
    row = lax.broadcasted_iota(jnp.int32, grad_ref.shape, 1)
    grad_ref[...] = jnp.where(row >= ID_ROW, rec_ref[...], grad_ref[...])


def final_kernel(own_ref, prev_ref, inbox_ref, move_ref, move_row_ref, out_ref, par_ref, sum_ref, res_ref):
    count = inbox_ref.shape[1] // ROWS
    for b in range(NBLK):
        here = own_ref[:, b * BLK : (b + 1) * BLK].astype(F32)
        there = prev_ref[:, b * BLK : (b + 1) * BLK].astype(F32)
        par_ref[pl.ds(b, PAR, stride=NBLK), :] = jnp.where(move_ref[b] == 1, there, here)
    cams = []
    for v in range(2):
        ids = inbox_ref[v, pl.ds(ID_ROW, count, stride=ROWS), :].astype(jnp.int32)
        passed = (lax.broadcasted_iota(jnp.int32, (count, BLK), 0) >= count // 2).astype(jnp.int32)
        hit = (ids == lax.broadcasted_iota(jnp.int32, (count, BLK), 1)) & (passed == move_row_ref[...])
        hit = hit.astype(F32)
        for k in range(9):
            values = inbox_ref[v, pl.ds(k, count, stride=ROWS), :]
            summed = lax.dot_general(
                hit, values, (((0,), (0,)), ((), ())),
                precision=lax.Precision.HIGHEST, preferred_element_type=F32,
            )
            sum_ref[v, k] = summed[:NBLK]
        row = inbox_ref[v, pl.ds(CAM_ROW, 1), :]
        cams.append([row[:, i : i + 1] for i in range(11)])

    def chunk(c, carry):
        at = pl.multiple_of(c * 8, 8)

        def par(k):
            return par_ref[pl.ds(k * NBLK + at, 8), :]

        position = [par(k) for k in range(3)]
        scales = [par(3 + k) for k in range(3)]
        quaternion = [par(6 + k) for k in range(4)]
        harmonic_grads = []
        shared = None
        from_const = None
        for v in range(2):
            cam, eye = (cams[v][:8], cams[v][8:])
            grads = [sum_ref[v, k, pl.ds(at, 8), :] for k in range(9)]
            basis, basis_back = jax.vjp(lambda p: basis_of(p, eye), position)
            live = []
            for ch in range(3):
                colour = total_of([basis[k] * par(11 + 16 * ch + k) for k in range(16)]) + 0.5
                live.append(grads[ch] * jnp.where(colour > 0.0, 1.0, jnp.where(colour == 0.0, 0.5, 0.0)))
            for ch in range(3):
                for k in range(16):
                    slope = basis[k] * live[ch]
                    if v == 0:
                        harmonic_grads.append(slope)
                    else:
                        res_ref[pl.ds((11 + 16 * ch + k) * NBLK + at, 8), :] = (
                            harmonic_grads[16 * ch + k] + slope
                        )
            basis_cot = [
                total_of([live[ch] * par(11 + 16 * ch + k) for ch in range(3)]) for k in range(16)
            ]
            moved = basis_back(basis_cot)[0]
            _, shape_back = jax.vjp(
                lambda p, s, q: shape_coefs(p, s, q, cam), position, scales, quaternion
            )
            p_grad, s_grad, q_grad = shape_back(grads[3:9])
            p_grad = [p_grad[i] + moved[i] for i in range(3)]
            every = p_grad + list(s_grad) + list(q_grad)
            shared = every if v == 0 else [shared[i] + every[i] for i in range(10)]
            from_const = grads[8] if v == 0 else from_const + grads[8]
        shared.append(from_const * jax.nn.sigmoid(-par(10)))
        for k in range(11):
            res_ref[pl.ds(k * NBLK + at, 8), :] = shared[k]
        return carry

    lax.fori_loop(0, NBLK // 8, chunk, 0)
    for b in range(NBLK):
        out_ref[:, b * BLK : (b + 1) * BLK] = res_ref[pl.ds(b, PAR, stride=NBLK), :]


VMEM = pl.BlockSpec(memory_space=pltpu.VMEM)
SMEM = pl.BlockSpec(memory_space=pltpu.SMEM)
LIMIT = 48 * 1024 * 1024


def monomials():
    side = jnp.arange(TSIDE, dtype=F32) - (TSIDE - 1) / 2.0
    x, y = (jnp.tile(side, TSIDE), jnp.repeat(side, TSIDE))
    rows = [x * x, y * y, x * y, x, y, jnp.ones_like(x)]
    return jnp.pad(jnp.stack(rows), ((3, ROWS - 9), (0, 0))).astype(BF16)


def shards(gaussians, camera, eye_point, send_lists, tile_lists, moving_blocks, image_grad):
    owners = lax.axis_size("render")
    slots = owners * CAP
    params = pltpu.CompilerParams(vmem_limit_bytes=LIMIT)
    cam_row = jnp.concatenate([camera, eye_point, jnp.zeros((1, BLK - 11), F32)], axis=1)
    route = [(i, (i + 1) % owners) for i in range(owners)]
    passed = lax.ppermute(gaussians, "render", route)
    own_records = pl.pallas_call(
        project_kernel,
        out_shape=jax.ShapeDtypeStruct((ROWS, NBLK, BLK), F32),
        in_specs=[VMEM, SMEM, VMEM],
        out_specs=VMEM,
        scratch_shapes=[pltpu.VMEM((PAR * NBLK, BLK), F32)],
        compiler_params=params,
        name="project",
    )(gaussians, cam_row, cam_row)
    chosen = jnp.minimum(send_lists[0, 0].reshape(-1), NBLK - 1)
    outgoing = jnp.moveaxis(jnp.take(own_records, chosen, axis=1, mode="clip"), 0, 1)
    records = lax.all_to_all(outgoing, "render", split_axis=0, concat_axis=0, tiled=True)
    tiles, entries = tile_lists.shape[1:]
    order = tile_lists[0].reshape(tiles, SEG, entries // SEG).swapaxes(1, 2).reshape(tiles, entries)
    cotangent = jnp.pad(image_grad[0].swapaxes(0, 1), ((0, 0), (0, ROWS - 3), (0, 0)))
    rendered, record_grads = pl.pallas_call(
        render_kernel,
        out_shape=[
            jax.ShapeDtypeStruct((3, tiles, PIX), F32),
            jax.ShapeDtypeStruct((slots, ROWS, BLK), F32),
        ],
        in_specs=[VMEM] * 4,
        out_specs=[VMEM] * 2,
        compiler_params=params,
        name="render",
    )(records, order, cotangent, monomials())
    grads = record_grads.reshape(owners, CAP * ROWS, BLK)
    both = jnp.stack([grads, jnp.roll(grads, 1, axis=0)], axis=1)
    received = lax.all_to_all(both, "render", split_axis=0, concat_axis=0, tiled=True)
    received = received.swapaxes(0, 1).reshape(2 * slots * ROWS, BLK)
    other = lax.ppermute(received, "view", [(0, 1), (1, 0)])
    inbox = jnp.stack([received, other])
    moving_row = jnp.pad(moving_blocks, (0, BLK - NBLK)).reshape(1, BLK)
    gradients = pl.pallas_call(
        final_kernel,
        out_shape=jax.ShapeDtypeStruct(gaussians.shape, F32),
        in_specs=[VMEM, VMEM, VMEM, SMEM, VMEM],
        out_specs=VMEM,
        scratch_shapes=[
            pltpu.VMEM((PAR * NBLK, BLK), F32),
            pltpu.VMEM((2, 9, NBLK, BLK), F32),
            pltpu.VMEM((PAR * NBLK, BLK), F32),
        ],
        compiler_params=params,
        name="finish",
    )(gaussians, passed, inbox, moving_blocks, moving_row)
    return (rendered[None], gradients)


def solution(mesh):
    in_specs = (
        P(None, ("groups", "render")),
        P(("groups", "view"), None),
        P(("groups", "view"), None),
        P(("groups", "view"), "render", None, None),
        P(("groups", "view"), "render", None),
        P("groups"),
        P(("groups", "view"), None, "render", None),
    )
    out_specs = (P(("groups", "view"), None, "render", None), P(None, ("groups", "render")))
    return jax.shard_map(shards, mesh=mesh, in_specs=in_specs, out_specs=out_specs, check_vma=False)
```

```python
import functools

import jax
import jax.numpy as jnp
from jax import lax
from jax.experimental import pallas as pl
from jax.experimental.pallas import tpu as pltpu
from jax.sharding import PartitionSpec as P

PAR = 59
BLK = 128
TSIDE = 16
PIX = TSIDE * TSIDE
NBLK = 32
CAP = 2
ROWS = 16
ID_ROW = 9
CAM_ROW = 10
SEG = 8

LOW_PASS = 0.3
SH_ZERO = 0.28209479177387814
SH_ONE = 0.4886025119029199
SH_TWO = (
    1.0925484305920792,
    -1.0925484305920792,
    0.31539156525252005,
    -1.0925484305920792,
    0.5462742152960396,
)
SH_THREE = (
    -0.5900435899266435,
    2.890611442640554,
    -0.4570457994644658,
    0.3731763325901154,
    -0.4570457994644658,
    1.445305721320277,
    -0.5900435899266435,
)
F32 = jnp.float32
BF16 = jnp.bfloat16
MESH = pl.DeviceIdType.MESH


def harmonics(x, y, z):
    xx, yy, zz = (x * x, y * y, z * z)
    return [
        SH_ZERO * jnp.ones_like(x),
        -SH_ONE * y,
        SH_ONE * z,
        -SH_ONE * x,
        SH_TWO[0] * x * y,
        SH_TWO[1] * y * z,
        SH_TWO[2] * (2.0 * zz - xx - yy),
        SH_TWO[3] * x * z,
        SH_TWO[4] * (xx - yy),
        SH_THREE[0] * y * (3.0 * xx - yy),
        SH_THREE[1] * x * y * z,
        SH_THREE[2] * y * (4.0 * zz - xx - yy),
        SH_THREE[3] * z * (2.0 * zz - 3.0 * xx - 3.0 * yy),
        SH_THREE[4] * x * (4.0 * zz - xx - yy),
        SH_THREE[5] * z * (xx - yy),
        SH_THREE[6] * x * (xx - 3.0 * yy),
    ]


def total_of(terms):
    total = terms[0]
    for term in terms[1:]:
        total = total + term
    return total


def shape_coefs(position, scales, quaternion, cam):
    variance = [jnp.exp(2.0 * s) for s in scales]
    inverse = 1.0 / jnp.sqrt(total_of([c * c for c in quaternion]))
    w, x, y, z = [c * inverse for c in quaternion]
    rotation = [
        [1.0 - 2.0 * (y * y + z * z), 2.0 * (x * y - w * z), 2.0 * (x * z + w * y)],
        [2.0 * (x * y + w * z), 1.0 - 2.0 * (x * x + z * z), 2.0 * (y * z - w * x)],
        [2.0 * (x * z - w * y), 2.0 * (y * z + w * x), 1.0 - 2.0 * (x * x + y * y)],
    ]
    mapped = [
        [total_of([cam[3 * a + i] * rotation[i][k] for i in range(3)]) for k in range(3)]
        for a in range(2)
    ]
    scaled = [mapped[0][k] * variance[k] for k in range(3)]
    cov_xx = total_of([scaled[k] * mapped[0][k] for k in range(3)]) + LOW_PASS
    cov_xy = total_of([scaled[k] * mapped[1][k] for k in range(3)])
    cov_yy = total_of([mapped[1][k] * mapped[1][k] * variance[k] for k in range(3)]) + LOW_PASS
    over = 1.0 / (cov_xx * cov_yy - cov_xy * cov_xy)
    conic_a, conic_b, conic_c = (cov_yy * over, -cov_xy * over, cov_xx * over)
    mean_x = total_of([cam[i] * position[i] for i in range(3)]) + cam[6]
    mean_y = total_of([cam[3 + i] * position[i] for i in range(3)]) + cam[7]
    lin_x = conic_a * mean_x + conic_b * mean_y
    lin_y = conic_b * mean_x + conic_c * mean_y
    const = -0.5 * (lin_x * mean_x + lin_y * mean_y)
    return [-0.5 * conic_a, -0.5 * conic_c, -conic_b, lin_x, lin_y, const]


def basis_of(position, eye):
    direction = [position[i] - eye[i] for i in range(3)]
    inverse = 1.0 / jnp.sqrt(total_of([c * c for c in direction]))
    return harmonics(*[c * inverse for c in direction])


def log_sigmoid(x):
    return jnp.minimum(x, 0.0) - jnp.log1p(jnp.exp(-jnp.abs(x)))


def lane_row(values):
    lane = lax.broadcasted_iota(jnp.int32, (1, BLK), 1)
    row = jnp.zeros((1, BLK), F32)
    for i, value in enumerate(values):
        row = jnp.where(lane == i, value, row)
    return row


def project_all(gauss_ref, cam_ref, eye_ref, rec_ref, par_ref):
    for b in range(NBLK):
        par_ref[pl.ds(b, PAR, stride=NBLK), :] = gauss_ref[:, b * BLK : (b + 1) * BLK].astype(F32)
    cam = [cam_ref[0, i] for i in range(8)]
    eye = [eye_ref[0, i] for i in range(3)]
    cam_row = jnp.broadcast_to(lane_row(cam + eye), (8, BLK))

    def chunk(c, carry):
        at = pl.multiple_of(c * 8, 8)

        def par(k):
            return par_ref[pl.ds(k * NBLK + at, 8), :]

        position = [par(k) for k in range(3)]
        coefs = shape_coefs(position, [par(3 + k) for k in range(3)], [par(6 + k) for k in range(4)], cam)
        coefs[5] = coefs[5] + log_sigmoid(par(10))
        basis = basis_of(position, eye)
        rows = []
        for ch in range(3):
            colour = total_of([basis[k] * par(11 + 16 * ch + k) for k in range(16)])
            rows.append(jnp.maximum(colour + 0.5, 0.0))
        rows += coefs
        rows.append((lax.broadcasted_iota(jnp.int32, (8, BLK), 0) + at).astype(F32))
        rows.append(cam_row)
        for k in range(ROWS):
            value = rows[k] if k < len(rows) else jnp.zeros((8, BLK), F32)
            rec_ref[pl.ds(at, 8), k, :] = value
        return carry

    lax.fori_loop(0, NBLK // 8, chunk, 0)


def split(values, count):
    pieces = []
    rest = values
    for i in range(count):
        piece = rest.astype(BF16)
        pieces.append(piece)
        if i + 1 < count:
            rest = rest - piece.astype(F32)
    return pieces


def dot_tn(a, b):
    return lax.dot_general(a, b, (((0,), (0,)), ((), ())), preferred_element_type=F32)


def dot_nt(a, b):
    return lax.dot_general(a, b, (((1,), (1,)), ((), ())), preferred_element_type=F32)


def dot_nn(a, b):
    return lax.dot_general(a, b, (((1,), (0,)), ((), ())), preferred_element_type=F32)


def monomials():
    pixel = lax.broadcasted_iota(jnp.int32, (1, PIX), 1)
    middle = (TSIDE - 1) / 2.0
    x = jnp.bitwise_and(pixel, TSIDE - 1).astype(F32) - middle
    y = jnp.right_shift(pixel, 4).astype(F32) - middle
    zero = jnp.zeros_like(x)
    rows = [zero] * 3 + [x * x, y * y, x * y, x, y, zero + 1.0] + [zero] * (ROWS - 9)
    return jnp.concatenate(rows, axis=0).astype(BF16)


def reorder(list_ref, order_ref):
    tiles, entries = list_ref.shape[1:]
    steps = entries // SEG
    for start in range(0, entries, BLK):
        place = lax.broadcasted_iota(jnp.int32, (tiles, BLK), 1) + start
        entry = jnp.bitwise_and(place, SEG - 1) * steps + place // SEG
        lanes = jnp.bitwise_and(entry, BLK - 1)
        found = jnp.zeros((tiles, BLK), jnp.int32)
        for first in range(0, entries, BLK):
            values = list_ref[0, :, first : first + BLK]
            taken = jnp.take_along_axis(values, lanes, axis=1, mode="promise_in_bounds")
            found = jnp.where(entry // BLK == first // BLK, taken, found)
        order_ref[:, start : start + BLK] = found


def render_all(rec_ref, order_ref, cot_ref, image_ref, grad_ref):
    slots = rec_ref.shape[0]
    tiles, entries = order_ref.shape
    group = min(slots, 16)
    grad_ref[...] = jnp.zeros_like(grad_ref)
    mono = monomials()
    mono_three = jnp.concatenate([mono, mono, mono], axis=0)

    def tile(t, carry):
        index = order_ref[pl.ds(t, 1), :]
        lane = jnp.bitwise_and(index, BLK - 1)
        slot = jnp.right_shift(index, 7)
        picked = []
        for start in range(0, entries, BLK):
            lanes = jnp.broadcast_to(lane[:, start : start + BLK], (ROWS, BLK))
            owner = jnp.broadcast_to(slot[:, start : start + BLK], (ROWS, BLK))

            def pick(s, found):
                taken = jnp.take_along_axis(rec_ref[s], lanes, axis=1, mode="promise_in_bounds")
                return jnp.where(owner == s, taken, found)

            found = jnp.zeros((ROWS, BLK), F32)
            if slots <= 16:
                for s in range(slots):
                    found = pick(s, found)
            else:
                found = lax.fori_loop(0, slots, pick, found)
            picked.append(found)
        records = jnp.concatenate(picked, axis=1)
        rec_three = jnp.concatenate(split(records, 3), axis=0)
        cot = [cot_ref[0, ch, pl.ds(t, 1), :] for ch in range(3)] + [jnp.zeros((ROWS - 3, PIX), F32)]
        cot_one, cot_two = split(jnp.concatenate(cot, axis=0), 2)
        power = dot_tn(rec_three, mono_three)
        toward = dot_tn(
            jnp.concatenate([rec_three, rec_three], axis=0),
            jnp.concatenate([cot_one] * 3 + [cot_two] * 3, axis=0),
        )
        steps = entries // SEG
        keep = jnp.ones((SEG, PIX), F32)
        seen = jnp.zeros((SEG, PIX), F32)
        alphas, weights = ([], [])
        for r in range(steps):
            alpha = jnp.exp(power[r * SEG : (r + 1) * SEG])
            weight = alpha * keep
            seen = seen + weight * toward[r * SEG : (r + 1) * SEG]
            keep = keep - weight
            alphas.append(alpha)
            weights.append(weight)
        front = [jnp.ones((1, PIX), F32)]
        for s in range(SEG - 1):
            front.append(front[-1] * keep[s : s + 1])
        behind = [jnp.zeros((1, PIX), F32)]
        for s in range(SEG - 1, 0, -1):
            behind.append(seen[s : s + 1] + keep[s : s + 1] * behind[-1])
        front = jnp.concatenate(front, axis=0)
        back = jnp.concatenate(behind[::-1], axis=0)
        slopes = [None] * steps
        for r in range(steps - 1, -1, -1):
            weight = weights[r] * front
            weights[r] = weight
            change = toward[r * SEG : (r + 1) * SEG] - back
            slopes[r] = weight * change
            back = back + alphas[r] * change
        weight_one, weight_two = split(jnp.concatenate(weights, axis=0), 2)
        slope_one, slope_two = split(jnp.concatenate(slopes, axis=0), 2)
        image = dot_nn(rec_three, weight_one) + dot_nn(rec_three, weight_two)
        image = image[:ROWS] + image[ROWS : 2 * ROWS] + image[2 * ROWS :]
        for ch in range(3):
            image_ref[0, ch, pl.ds(t, 1), :] = image[ch : ch + 1]
        cot_both = jnp.concatenate([cot_one, cot_two], axis=0)
        colour_grad = dot_nt(cot_both, weight_one) + dot_nt(cot_both, weight_two)
        shape_grad = dot_nt(mono, slope_one) + dot_nt(mono, slope_two)
        entry_grad = colour_grad[:ROWS] + colour_grad[ROWS:] + shape_grad
        pieces = split(entry_grad, 2)
        where_lane = lax.broadcasted_iota(jnp.int32, (BLK, entries), 0) == lane
        where_lane = where_lane.astype(F32).astype(BF16)

        def spread(first, carry):
            total = None
            masks = [(slot == first + s).astype(F32).astype(BF16) for s in range(group)]
            for piece in pieces:
                stacked = jnp.concatenate([piece * mask for mask in masks], axis=0)
                part = dot_nt(stacked, where_lane)
                total = part if total is None else total + part
            grad_ref[pl.ds(first, group)] += total.reshape(group, ROWS, BLK)
            return carry

        if slots == group:
            spread(0, 0)
        else:
            lax.fori_loop(0, slots // group, lambda i, c: spread(i * group, c), 0)
        return carry

    lax.fori_loop(0, tiles, tile, 0)
    row = lax.broadcasted_iota(jnp.int32, grad_ref.shape, 1)
    grad_ref[...] = jnp.where(row >= ID_ROW, rec_ref[...], grad_ref[...])


def each(count, body):
    if count <= 16:
        for i in range(count):
            body(i)
    else:
        lax.fori_loop(0, count, lambda i, carry: (body(i), carry)[1], 0)


def scene_kernel(
    owners, views, gauss_ref, cam_ref, eye_ref, send_ref, list_ref, cot_ref,
    image_ref, back_ref, passed_ref,
    par_ref, rec_ref, out_ref, in_ref, order_ref, grad_ref, ext_ref,
    pass_send, pass_recv, rec_send, rec_recv, back_send, back_recv,
):
    me = lax.axis_index("render")
    view = lax.axis_index("view")
    peers = owners * views
    mine = me * views + view
    barrier = pltpu.get_barrier_semaphore()

    def at(peer):
        return {"render": peer // views, "view": peer % views}

    def greet(i):
        pl.semaphore_signal(barrier, inc=1, device_id=at((mine + 1 + i) % peers), device_id_type=MESH)

    each(peers - 1, greet)
    project_all(gauss_ref, cam_ref, eye_ref, rec_ref, par_ref)

    def fill(i):
        for c in range(CAP):
            block = jnp.minimum(send_ref[0, 0, i, c], NBLK - 1)
            out_ref[i, c] = rec_ref[block]

    each(owners, fill)
    pl.semaphore_wait(barrier, peers - 1)

    def record_copy(i):
        peer = (me + 1 + i) % owners
        return pltpu.make_async_remote_copy(
            src_ref=out_ref.at[peer], dst_ref=in_ref.at[me],
            send_sem=rec_send.at[i], recv_sem=rec_recv.at[i],
            device_id={"render": peer}, device_id_type=MESH,
        )

    each(owners - 1, lambda i: record_copy(i).start())
    passing = pltpu.make_async_remote_copy(
        src_ref=gauss_ref, dst_ref=passed_ref, send_sem=pass_send, recv_sem=pass_recv,
        device_id={"render": (me + 1) % owners}, device_id_type=MESH,
    )
    passing.start()
    in_ref[me] = out_ref[me]
    reorder(list_ref, order_ref)
    each(owners - 1, lambda i: record_copy(i).wait())
    render_all(in_ref.reshape(owners * CAP, ROWS, BLK), order_ref, cot_ref, image_ref, grad_ref)
    ext_ref[pl.ds(1, owners)] = grad_ref[...].reshape(owners, CAP, ROWS, BLK)
    ext_ref[0] = ext_ref[owners]

    def back_copy(i):
        peer = (mine + 1 + i) % peers
        return pltpu.make_async_remote_copy(
            src_ref=ext_ref.at[pl.ds(peer // views, 2)], dst_ref=back_ref.at[view, me],
            send_sem=back_send.at[i], recv_sem=back_recv.at[i],
            device_id=at(peer), device_id_type=MESH,
        )

    each(peers - 1, lambda i: back_copy(i).start())
    back_ref[view, me] = ext_ref[pl.ds(me, 2)]
    each(peers - 1, lambda i: back_copy(i).wait())
    passing.wait()


def final_kernel(own_ref, prev_ref, inbox_ref, move_ref, out_ref, par_ref, sum_ref, res_ref):
    count = inbox_ref.shape[1] // ROWS
    for b in range(NBLK):
        here = own_ref[:, b * BLK : (b + 1) * BLK].astype(F32)
        there = prev_ref[:, b * BLK : (b + 1) * BLK].astype(F32)
        par_ref[pl.ds(b, PAR, stride=NBLK), :] = jnp.where(move_ref[b] == 1, there, here)
    cams = []
    move_row = lane_row([move_ref[b].astype(F32) for b in range(NBLK)])
    from_prev = jnp.bitwise_and(lax.broadcasted_iota(jnp.int32, (count, BLK), 0) // CAP, 1) == 0
    wanted = from_prev.astype(F32) == move_row
    for v in range(2):
        ids = inbox_ref[v, pl.ds(ID_ROW, count, stride=ROWS), :].astype(jnp.int32)
        hit = (ids == lax.broadcasted_iota(jnp.int32, (count, BLK), 1)) & wanted
        hit = hit.astype(F32)
        for k in range(9):
            values = inbox_ref[v, pl.ds(k, count, stride=ROWS), :]
            summed = lax.dot_general(
                hit, values, (((0,), (0,)), ((), ())),
                precision=lax.Precision.HIGHEST, preferred_element_type=F32,
            )
            sum_ref[v, k] = summed[:NBLK]
        row = inbox_ref[v, pl.ds(CAM_ROW, 1), :]
        cams.append([row[:, i : i + 1] for i in range(11)])

    def chunk(c, carry):
        at = pl.multiple_of(c * 8, 8)

        def par(k):
            return par_ref[pl.ds(k * NBLK + at, 8), :]

        position = [par(k) for k in range(3)]
        scales = [par(3 + k) for k in range(3)]
        quaternion = [par(6 + k) for k in range(4)]
        harmonic_grads = []
        shared = None
        from_const = None
        for v in range(2):
            cam, eye = (cams[v][:8], cams[v][8:])
            grads = [sum_ref[v, k, pl.ds(at, 8), :] for k in range(9)]
            basis, basis_back = jax.vjp(lambda p: basis_of(p, eye), position)
            live = []
            for ch in range(3):
                colour = total_of([basis[k] * par(11 + 16 * ch + k) for k in range(16)]) + 0.5
                live.append(grads[ch] * jnp.where(colour > 0.0, 1.0, jnp.where(colour == 0.0, 0.5, 0.0)))
            for ch in range(3):
                for k in range(16):
                    slope = basis[k] * live[ch]
                    if v == 0:
                        harmonic_grads.append(slope)
                    else:
                        res_ref[pl.ds((11 + 16 * ch + k) * NBLK + at, 8), :] = (
                            harmonic_grads[16 * ch + k] + slope
                        )
            basis_cot = [
                total_of([live[ch] * par(11 + 16 * ch + k) for ch in range(3)]) for k in range(16)
            ]
            moved = basis_back(basis_cot)[0]
            _, shape_back = jax.vjp(
                lambda p, s, q: shape_coefs(p, s, q, cam), position, scales, quaternion
            )
            p_grad, s_grad, q_grad = shape_back(grads[3:9])
            p_grad = [p_grad[i] + moved[i] for i in range(3)]
            every = p_grad + list(s_grad) + list(q_grad)
            shared = every if v == 0 else [shared[i] + every[i] for i in range(10)]
            from_const = grads[8] if v == 0 else from_const + grads[8]
        shared.append(from_const * jax.nn.sigmoid(-par(10)))
        for k in range(11):
            res_ref[pl.ds(k * NBLK + at, 8), :] = shared[k]
        return carry

    lax.fori_loop(0, NBLK // 8, chunk, 0)
    for b in range(NBLK):
        out_ref[:, b * BLK : (b + 1) * BLK] = res_ref[pl.ds(b, PAR, stride=NBLK), :]


VMEM = pl.BlockSpec(memory_space=pltpu.VMEM)
SMEM = pl.BlockSpec(memory_space=pltpu.SMEM)
LIMIT = 48 * 1024 * 1024


def shards(gaussians, camera, eye_point, send_lists, tile_lists, moving_blocks, image_grad):
    owners = lax.axis_size("render")
    views = lax.axis_size("view")
    slots = owners * CAP
    tiles, entries = tile_lists.shape[1:]
    dma = pltpu.SemaphoreType.DMA
    rendered, back, passed = pl.pallas_call(
        functools.partial(scene_kernel, owners, views),
        out_shape=[
            jax.ShapeDtypeStruct(image_grad.shape, F32),
            jax.ShapeDtypeStruct((views, owners, 2, CAP, ROWS, BLK), F32),
            jax.ShapeDtypeStruct(gaussians.shape, BF16),
        ],
        in_specs=[VMEM, SMEM, SMEM, SMEM, VMEM, VMEM],
        out_specs=[VMEM] * 3,
        scratch_shapes=[
            pltpu.VMEM((PAR * NBLK, BLK), F32),
            pltpu.VMEM((NBLK, ROWS, BLK), F32),
            pltpu.VMEM((owners, CAP, ROWS, BLK), F32),
            pltpu.VMEM((owners, CAP, ROWS, BLK), F32),
            pltpu.VMEM((tiles, entries), jnp.int32),
            pltpu.VMEM((slots, ROWS, BLK), F32),
            pltpu.VMEM((owners + 1, CAP, ROWS, BLK), F32),
            dma, dma,
            dma((owners - 1,)), dma((owners - 1,)),
            dma((owners * views - 1,)), dma((owners * views - 1,)),
        ],
        compiler_params=pltpu.CompilerParams(
            vmem_limit_bytes=LIMIT, collective_id=0, has_side_effects=True
        ),
        name="scene",
    )(gaussians, camera, eye_point, send_lists, tile_lists, image_grad)
    inbox = back.reshape(views, owners * 2 * CAP * ROWS, BLK)
    gradients = pl.pallas_call(
        final_kernel,
        out_shape=jax.ShapeDtypeStruct(gaussians.shape, F32),
        in_specs=[VMEM, VMEM, VMEM, SMEM],
        out_specs=VMEM,
        scratch_shapes=[
            pltpu.VMEM((PAR * NBLK, BLK), F32),
            pltpu.VMEM((2, 9, NBLK, BLK), F32),
            pltpu.VMEM((PAR * NBLK, BLK), F32),
        ],
        compiler_params=pltpu.CompilerParams(vmem_limit_bytes=LIMIT),
        name="finish",
    )(gaussians, passed, inbox, moving_blocks)
    return (rendered, gradients)


def solution(mesh):
    in_specs = (
        P(None, ("groups", "render")),
        P(("groups", "view"), None),
        P(("groups", "view"), None),
        P(("groups", "view"), "render", None, None),
        P(("groups", "view"), "render", None),
        P("groups"),
        P(("groups", "view"), None, "render", None),
    )
    out_specs = (P(("groups", "view"), None, "render", None), P(None, ("groups", "render")))
    return jax.shard_map(shards, mesh=mesh, in_specs=in_specs, out_specs=out_specs, check_vma=False)
```

```python
import functools

import jax
import jax.numpy as jnp
from jax import lax
from jax.experimental import pallas as pl
from jax.experimental.pallas import tpu as pltpu
from jax.sharding import PartitionSpec as P

PAR = 59
BLK = 128
TSIDE = 16
PIX = TSIDE * TSIDE
NBLK = 32
CAP = 2
ROWS = 16
ID_ROW = 9
SENT = 10
CAM_LANE = NBLK
SEG = 8
TOGETHER = 2

LOW_PASS = 0.3
SH_ZERO = 0.28209479177387814
SH_ONE = 0.4886025119029199
SH_TWO = (
    1.0925484305920792,
    -1.0925484305920792,
    0.31539156525252005,
    -1.0925484305920792,
    0.5462742152960396,
)
SH_THREE = (
    -0.5900435899266435,
    2.890611442640554,
    -0.4570457994644658,
    0.3731763325901154,
    -0.4570457994644658,
    1.445305721320277,
    -0.5900435899266435,
)
F32 = jnp.float32
BF16 = jnp.bfloat16
MESH = pl.DeviceIdType.MESH


def harmonics(x, y, z):
    xx, yy, zz = (x * x, y * y, z * z)
    return [
        SH_ZERO * jnp.ones_like(x),
        -SH_ONE * y,
        SH_ONE * z,
        -SH_ONE * x,
        SH_TWO[0] * x * y,
        SH_TWO[1] * y * z,
        SH_TWO[2] * (2.0 * zz - xx - yy),
        SH_TWO[3] * x * z,
        SH_TWO[4] * (xx - yy),
        SH_THREE[0] * y * (3.0 * xx - yy),
        SH_THREE[1] * x * y * z,
        SH_THREE[2] * y * (4.0 * zz - xx - yy),
        SH_THREE[3] * z * (2.0 * zz - 3.0 * xx - 3.0 * yy),
        SH_THREE[4] * x * (4.0 * zz - xx - yy),
        SH_THREE[5] * z * (xx - yy),
        SH_THREE[6] * x * (xx - 3.0 * yy),
    ]


def total_of(terms):
    total = terms[0]
    for term in terms[1:]:
        total = total + term
    return total


def shape_coefs(position, scales, quaternion, cam):
    variance = [jnp.exp(2.0 * s) for s in scales]
    inverse = 1.0 / jnp.sqrt(total_of([c * c for c in quaternion]))
    w, x, y, z = [c * inverse for c in quaternion]
    rotation = [
        [1.0 - 2.0 * (y * y + z * z), 2.0 * (x * y - w * z), 2.0 * (x * z + w * y)],
        [2.0 * (x * y + w * z), 1.0 - 2.0 * (x * x + z * z), 2.0 * (y * z - w * x)],
        [2.0 * (x * z - w * y), 2.0 * (y * z + w * x), 1.0 - 2.0 * (x * x + y * y)],
    ]
    mapped = [
        [total_of([cam[3 * a + i] * rotation[i][k] for i in range(3)]) for k in range(3)]
        for a in range(2)
    ]
    scaled = [mapped[0][k] * variance[k] for k in range(3)]
    cov_xx = total_of([scaled[k] * mapped[0][k] for k in range(3)]) + LOW_PASS
    cov_xy = total_of([scaled[k] * mapped[1][k] for k in range(3)])
    cov_yy = total_of([mapped[1][k] * mapped[1][k] * variance[k] for k in range(3)]) + LOW_PASS
    over = 1.0 / (cov_xx * cov_yy - cov_xy * cov_xy)
    conic_a, conic_b, conic_c = (cov_yy * over, -cov_xy * over, cov_xx * over)
    mean_x = total_of([cam[i] * position[i] for i in range(3)]) + cam[6]
    mean_y = total_of([cam[3 + i] * position[i] for i in range(3)]) + cam[7]
    lin_x = conic_a * mean_x + conic_b * mean_y
    lin_y = conic_b * mean_x + conic_c * mean_y
    const = -0.5 * (lin_x * mean_x + lin_y * mean_y)
    return [-0.5 * conic_a, -0.5 * conic_c, -conic_b, lin_x, lin_y, const]


def basis_of(position, eye):
    direction = [position[i] - eye[i] for i in range(3)]
    inverse = 1.0 / jnp.sqrt(total_of([c * c for c in direction]))
    return harmonics(*[c * inverse for c in direction])


def log_sigmoid(x):
    return jnp.minimum(x, 0.0) - jnp.log1p(jnp.exp(-jnp.abs(x)))


def lane_row(values):
    lane = lax.broadcasted_iota(jnp.int32, (1, BLK), 1)
    row = jnp.zeros((1, BLK), F32)
    for i, value in enumerate(values):
        row = jnp.where(lane == i, value, row)
    return row


def project_all(gauss_ref, cam_ref, eye_ref, rec_ref, par_ref):
    for b in range(NBLK):
        par_ref[pl.ds(b, PAR, stride=NBLK), :] = gauss_ref[:, b * BLK : (b + 1) * BLK].astype(F32)
    cam = [cam_ref[0, i] for i in range(8)]
    eye = [eye_ref[0, i] for i in range(3)]
    cam_row = jnp.broadcast_to(lane_row([0.0] * CAM_LANE + cam + eye), (8, BLK))
    is_id = lax.broadcasted_iota(jnp.int32, (8, BLK), 1) < CAM_LANE

    def chunk(c, carry):
        at = pl.multiple_of(c * 8, 8)

        def par(k):
            return par_ref[pl.ds(k * NBLK + at, 8), :]

        position = [par(k) for k in range(3)]
        coefs = shape_coefs(position, [par(3 + k) for k in range(3)], [par(6 + k) for k in range(4)], cam)
        coefs[5] = coefs[5] + log_sigmoid(par(10))
        basis = basis_of(position, eye)
        rows = []
        for ch in range(3):
            colour = total_of([basis[k] * par(11 + 16 * ch + k) for k in range(16)])
            rows.append(jnp.maximum(colour + 0.5, 0.0))
        rows += coefs
        block_id = (lax.broadcasted_iota(jnp.int32, (8, BLK), 0) + at).astype(F32)
        rows.append(jnp.where(is_id, block_id, cam_row))
        for k in range(ROWS):
            value = rows[k] if k < len(rows) else jnp.zeros((8, BLK), F32)
            rec_ref[pl.ds(at, 8), k, :] = value
        return carry

    lax.fori_loop(0, NBLK // 8, chunk, 0)


def split(values, count):
    pieces = []
    rest = values
    for i in range(count):
        piece = rest.astype(BF16)
        pieces.append(piece)
        if i + 1 < count:
            rest = rest - piece.astype(F32)
    return pieces


def dot_tn(a, b):
    return lax.dot_general(a, b, (((0,), (0,)), ((), ())), preferred_element_type=F32)


def dot_nt(a, b):
    return lax.dot_general(a, b, (((1,), (1,)), ((), ())), preferred_element_type=F32)


def dot_nn(a, b):
    return lax.dot_general(a, b, (((1,), (0,)), ((), ())), preferred_element_type=F32)


def monomials():
    pixel = lax.broadcasted_iota(jnp.int32, (1, PIX), 1)
    middle = (TSIDE - 1) / 2.0
    x = jnp.bitwise_and(pixel, TSIDE - 1).astype(F32) - middle
    y = jnp.right_shift(pixel, 4).astype(F32) - middle
    zero = jnp.zeros_like(x)
    rows = [zero] * 3 + [x * x, y * y, x * y, x, y, zero + 1.0] + [zero] * (ROWS - 9)
    return jnp.concatenate(rows, axis=0).astype(BF16)


def reorder(list_ref, order_ref):
    tiles, entries = list_ref.shape[1:]
    steps = entries // SEG
    for start in range(0, entries, BLK):
        place = lax.broadcasted_iota(jnp.int32, (tiles, BLK), 1) + start
        entry = jnp.bitwise_and(place, SEG - 1) * steps + place // SEG
        lanes = jnp.bitwise_and(entry, BLK - 1)
        found = jnp.zeros((tiles, BLK), jnp.int32)
        for first in range(0, entries, BLK):
            values = list_ref[0, :, first : first + BLK]
            taken = jnp.take_along_axis(values, lanes, axis=1, mode="promise_in_bounds")
            found = jnp.where(entry // BLK == first // BLK, taken, found)
        order_ref[:, start : start + BLK] = found


def render_all(rec_ref, order_ref, cot_ref, image_ref, grad_ref):
    slots = rec_ref.shape[0]
    tiles, entries = order_ref.shape
    group = min(slots, 16)
    grad_ref[...] = jnp.zeros_like(grad_ref)
    mono = monomials()
    mono_three = jnp.concatenate([mono, mono, mono], axis=0)

    def tile(t):
        index = order_ref[pl.ds(t, 1), :]
        lane = jnp.bitwise_and(index, BLK - 1)
        slot = jnp.right_shift(index, 7)
        picked = []
        for start in range(0, entries, BLK):
            lanes = jnp.broadcast_to(lane[:, start : start + BLK], (ROWS, BLK))
            owner = jnp.broadcast_to(slot[:, start : start + BLK], (ROWS, BLK))

            def pick(s, found):
                taken = jnp.take_along_axis(rec_ref[s], lanes, axis=1, mode="promise_in_bounds")
                return jnp.where(owner == s, taken, found)

            found = jnp.zeros((ROWS, BLK), F32)
            if slots <= 16:
                for s in range(slots):
                    found = pick(s, found)
            else:
                found = lax.fori_loop(0, slots, pick, found)
            picked.append(found)
        records = jnp.concatenate(picked, axis=1)
        rec_three = jnp.concatenate(split(records, 3), axis=0)
        cot = [cot_ref[0, ch, pl.ds(t, 1), :] for ch in range(3)] + [jnp.zeros((ROWS - 3, PIX), F32)]
        cot_one, cot_two = split(jnp.concatenate(cot, axis=0), 2)
        power = dot_tn(rec_three, mono_three)
        toward = dot_tn(
            jnp.concatenate([rec_three, rec_three], axis=0),
            jnp.concatenate([cot_one] * 3 + [cot_two] * 3, axis=0),
        )
        steps = entries // SEG
        keep = jnp.ones((SEG, PIX), F32)
        seen = jnp.zeros((SEG, PIX), F32)
        alphas, weights = ([], [])
        for r in range(steps):
            alpha = jnp.exp(power[r * SEG : (r + 1) * SEG])
            weight = alpha * keep
            seen = seen + weight * toward[r * SEG : (r + 1) * SEG]
            keep = keep * (1.0 - alpha)
            alphas.append(alpha)
            weights.append(weight)
        front = [jnp.ones((1, PIX), F32)]
        for s in range(SEG - 1):
            front.append(front[-1] * keep[s : s + 1])
        behind = [jnp.zeros((1, PIX), F32)]
        for s in range(SEG - 1, 0, -1):
            behind.append(seen[s : s + 1] + keep[s : s + 1] * behind[-1])
        front = jnp.concatenate(front, axis=0)
        back = jnp.concatenate(behind[::-1], axis=0)
        slopes = [None] * steps
        for r in range(steps - 1, -1, -1):
            weight = weights[r] * front
            weights[r] = weight
            value = toward[r * SEG : (r + 1) * SEG]
            slopes[r] = weight * (value - back)
            back = alphas[r] * value + (1.0 - alphas[r]) * back
        weight_one, weight_two = split(jnp.concatenate(weights, axis=0), 2)
        slope_one, slope_two = split(jnp.concatenate(slopes, axis=0), 2)
        image = dot_nn(rec_three, weight_one) + dot_nn(rec_three, weight_two)
        image = image[:ROWS] + image[ROWS : 2 * ROWS] + image[2 * ROWS :]
        for ch in range(3):
            image_ref[0, ch, pl.ds(t, 1), :] = image[ch : ch + 1]
        cot_both = jnp.concatenate([cot_one, cot_two], axis=0)
        colour_grad = dot_nt(cot_both, weight_one) + dot_nt(cot_both, weight_two)
        shape_grad = dot_nt(mono, slope_one) + dot_nt(mono, slope_two)
        entry_grad = colour_grad[:ROWS] + colour_grad[ROWS:] + shape_grad
        return split(entry_grad, 2), lane, slot

    together = TOGETHER if tiles % TOGETHER == 0 else 1

    def some_tiles(t, carry):
        drawn = [tile(t * together + i) for i in range(together)]
        pieces = [jnp.concatenate([d[0][i] for d in drawn], axis=1) for i in range(2)]
        lane = jnp.concatenate([d[1] for d in drawn], axis=1)
        slot = jnp.concatenate([d[2] for d in drawn], axis=1)
        here = lax.broadcasted_iota(jnp.int32, (BLK, lane.shape[1]), 0) == lane
        here = here.astype(F32).astype(BF16)

        def spread(first, carry):
            masks = [(slot == first + s).astype(F32).astype(BF16) for s in range(group)]
            parts = [
                dot_nt(jnp.concatenate([piece * mask for mask in masks], axis=0), here)
                for piece in pieces
            ]
            grad_ref[pl.ds(first, group)] += (parts[0] + parts[1]).reshape(group, ROWS, BLK)
            return carry

        if slots == group:
            spread(0, 0)
        else:
            lax.fori_loop(0, slots // group, lambda i, c: spread(i * group, c), 0)
        return carry

    lax.fori_loop(0, tiles // together, some_tiles, 0)
    row = lax.broadcasted_iota(jnp.int32, grad_ref.shape, 1)
    grad_ref[...] = jnp.where(row >= ID_ROW, rec_ref[...], grad_ref[...])


def each(count, body):
    if count <= 16:
        for i in range(count):
            body(i)
    else:
        lax.fori_loop(0, count, lambda i, carry: (body(i), carry)[1], 0)


def scene_kernel(
    owners, gauss_ref, cam_ref, eye_ref, send_ref, list_ref, cot_ref,
    image_ref, back_ref, passed_ref,
    par_ref, rec_ref, out_ref, in_ref, order_ref, grad_ref, ext_ref,
    pass_send, pass_recv, rec_send, rec_recv, back_send, back_recv, view_send, view_recv,
):
    me = lax.axis_index("render")
    view = lax.axis_index("view")
    barrier = pltpu.get_barrier_semaphore()

    def greet(i):
        pl.semaphore_signal(
            barrier, inc=1, device_id={"render": (me + 1 + i) % owners}, device_id_type=MESH
        )

    in_ref[...] = jnp.zeros_like(in_ref)
    each(owners - 1, greet)
    pl.semaphore_signal(barrier, inc=1, device_id={"view": 1 - view}, device_id_type=MESH)
    project_all(gauss_ref, cam_ref, eye_ref, rec_ref, par_ref)

    def fill(i):
        for c in range(CAP):
            block = jnp.minimum(send_ref[0, 0, i, c], NBLK - 1)
            out_ref[i, c] = rec_ref[block]

    each(owners, fill)
    pl.semaphore_wait(barrier, owners)

    def record_copy(i):
        peer = (me + 1 + i) % owners
        return pltpu.make_async_remote_copy(
            src_ref=out_ref.at[peer, :, pl.ds(0, SENT)], dst_ref=in_ref.at[me, :, pl.ds(0, SENT)],
            send_sem=rec_send.at[i], recv_sem=rec_recv.at[i],
            device_id={"render": peer}, device_id_type=MESH,
        )

    each(owners - 1, lambda i: record_copy(i).start())
    passing = pltpu.make_async_remote_copy(
        src_ref=gauss_ref, dst_ref=passed_ref, send_sem=pass_send, recv_sem=pass_recv,
        device_id={"render": (me + 1) % owners}, device_id_type=MESH,
    )
    in_ref[me] = out_ref[me]
    reorder(list_ref, order_ref)
    each(owners - 1, lambda i: record_copy(i).wait())
    passing.start()
    render_all(in_ref.reshape(owners * CAP, ROWS, BLK), order_ref, cot_ref, image_ref, grad_ref)
    ext_ref[pl.ds(1, owners)] = grad_ref[...].reshape(owners, CAP, ROWS, BLK)
    ext_ref[0] = ext_ref[owners]

    def back_copy(i):
        peer = (me + 1 + i) % owners
        return pltpu.make_async_remote_copy(
            src_ref=ext_ref.at[pl.ds(peer, 2), :, pl.ds(0, SENT)],
            dst_ref=back_ref.at[view, me, :, :, pl.ds(0, SENT)],
            send_sem=back_send.at[i], recv_sem=back_recv.at[i],
            device_id={"render": peer}, device_id_type=MESH,
        )

    def view_copy(i):
        source = (me + owners - i) % owners
        piece = back_ref.at[view, source, :, :, pl.ds(0, SENT)]
        return pltpu.make_async_remote_copy(
            src_ref=piece, dst_ref=piece,
            send_sem=view_send.at[i], recv_sem=view_recv.at[i],
            device_id={"view": 1 - view}, device_id_type=MESH,
        )

    def forward(i):
        back_copy(i).wait_recv()
        view_copy(i + 1).start()

    def settle(i):
        back_copy(i).wait_send()

    each(owners - 1, lambda i: back_copy(i).start())
    back_ref[view, me] = ext_ref[pl.ds(me, 2)]
    view_copy(0).start()
    each(owners - 1, forward)
    each(owners - 1, settle)
    each(owners, lambda i: view_copy(i).wait())
    passing.wait()


def final_kernel(own_ref, prev_ref, inbox_ref, move_ref, out_ref, par_ref, sum_ref, res_ref):
    count = inbox_ref.shape[1] // ROWS
    for b in range(NBLK):
        here = own_ref[:, b * BLK : (b + 1) * BLK].astype(F32)
        there = prev_ref[:, b * BLK : (b + 1) * BLK].astype(F32)
        par_ref[pl.ds(b, PAR, stride=NBLK), :] = jnp.where(move_ref[b] == 1, there, here)
    cams = []
    move_row = lane_row([move_ref[b].astype(F32) for b in range(NBLK)])
    from_prev = jnp.bitwise_and(lax.broadcasted_iota(jnp.int32, (count, BLK), 0) // CAP, 1) == 0
    wanted = from_prev.astype(F32) == move_row
    for v in range(2):
        ids = inbox_ref[v, pl.ds(ID_ROW, count, stride=ROWS), :].astype(jnp.int32)
        hit = (ids == lax.broadcasted_iota(jnp.int32, (count, BLK), 1)) & wanted
        hit = hit.astype(F32).astype(BF16)[:, :NBLK]
        values = jnp.concatenate(
            [inbox_ref[v, pl.ds(k, count, stride=ROWS), :] for k in range(9)], axis=1
        )
        summed = dot_tn(jnp.concatenate([hit] * 3, axis=0), jnp.concatenate(split(values, 3), axis=0))
        for k in range(9):
            sum_ref[v, k] = summed[:, k * BLK : (k + 1) * BLK]
        row = inbox_ref[v, pl.ds(ID_ROW, 1), :]
        cams.append([row[:, CAM_LANE + i : CAM_LANE + i + 1] for i in range(11)])

    def chunk(c, carry):
        at = pl.multiple_of(c * 8, 8)

        def par(k):
            return par_ref[pl.ds(k * NBLK + at, 8), :]

        position = [par(k) for k in range(3)]
        scales = [par(3 + k) for k in range(3)]
        quaternion = [par(6 + k) for k in range(4)]
        harmonic_grads = []
        shared = None
        from_const = None
        for v in range(2):
            cam, eye = (cams[v][:8], cams[v][8:])
            grads = [sum_ref[v, k, pl.ds(at, 8), :] for k in range(9)]
            basis, basis_back = jax.vjp(lambda p: basis_of(p, eye), position)
            live = []
            for ch in range(3):
                colour = total_of([basis[k] * par(11 + 16 * ch + k) for k in range(16)]) + 0.5
                live.append(grads[ch] * jnp.where(colour > 0.0, 1.0, jnp.where(colour == 0.0, 0.5, 0.0)))
            for ch in range(3):
                for k in range(16):
                    slope = basis[k] * live[ch]
                    if v == 0:
                        harmonic_grads.append(slope)
                    else:
                        res_ref[pl.ds((11 + 16 * ch + k) * NBLK + at, 8), :] = (
                            harmonic_grads[16 * ch + k] + slope
                        )
            basis_cot = [
                total_of([live[ch] * par(11 + 16 * ch + k) for ch in range(3)]) for k in range(16)
            ]
            moved = basis_back(basis_cot)[0]
            _, shape_back = jax.vjp(
                lambda p, s, q: shape_coefs(p, s, q, cam), position, scales, quaternion
            )
            p_grad, s_grad, q_grad = shape_back(grads[3:9])
            p_grad = [p_grad[i] + moved[i] for i in range(3)]
            every = p_grad + list(s_grad) + list(q_grad)
            shared = every if v == 0 else [shared[i] + every[i] for i in range(10)]
            from_const = grads[8] if v == 0 else from_const + grads[8]
        shared.append(from_const * jax.nn.sigmoid(-par(10)))
        for k in range(11):
            res_ref[pl.ds(k * NBLK + at, 8), :] = shared[k]
        return carry

    lax.fori_loop(0, NBLK // 8, chunk, 0)
    for b in range(NBLK):
        out_ref[:, b * BLK : (b + 1) * BLK] = res_ref[pl.ds(b, PAR, stride=NBLK), :]


VMEM = pl.BlockSpec(memory_space=pltpu.VMEM)
SMEM = pl.BlockSpec(memory_space=pltpu.SMEM)
LIMIT = 48 * 1024 * 1024


def shards(gaussians, camera, eye_point, send_lists, tile_lists, moving_blocks, image_grad):
    owners = lax.axis_size("render")
    views = lax.axis_size("view")
    slots = owners * CAP
    tiles, entries = tile_lists.shape[1:]
    dma = pltpu.SemaphoreType.DMA
    rendered, back, passed = pl.pallas_call(
        functools.partial(scene_kernel, owners),
        out_shape=[
            jax.ShapeDtypeStruct(image_grad.shape, F32),
            jax.ShapeDtypeStruct((views, owners, 2, CAP, ROWS, BLK), F32),
            jax.ShapeDtypeStruct(gaussians.shape, BF16),
        ],
        in_specs=[VMEM, SMEM, SMEM, SMEM, VMEM, VMEM],
        out_specs=[VMEM] * 3,
        scratch_shapes=[
            pltpu.VMEM((PAR * NBLK, BLK), F32),
            pltpu.VMEM((NBLK, ROWS, BLK), F32),
            pltpu.VMEM((owners, CAP, ROWS, BLK), F32),
            pltpu.VMEM((owners, CAP, ROWS, BLK), F32),
            pltpu.VMEM((tiles, entries), jnp.int32),
            pltpu.VMEM((slots, ROWS, BLK), F32),
            pltpu.VMEM((owners + 1, CAP, ROWS, BLK), F32),
            dma, dma,
            dma((owners - 1,)), dma((owners - 1,)),
            dma((owners - 1,)), dma((owners - 1,)),
            dma((owners,)), dma((owners,)),
        ],
        compiler_params=pltpu.CompilerParams(
            vmem_limit_bytes=LIMIT, collective_id=0, has_side_effects=True
        ),
        name="scene",
    )(gaussians, camera, eye_point, send_lists, tile_lists, image_grad)
    inbox = back.reshape(views, owners * 2 * CAP * ROWS, BLK)
    gradients = pl.pallas_call(
        final_kernel,
        out_shape=jax.ShapeDtypeStruct(gaussians.shape, F32),
        in_specs=[VMEM, VMEM, VMEM, SMEM],
        out_specs=VMEM,
        scratch_shapes=[
            pltpu.VMEM((PAR * NBLK, BLK), F32),
            pltpu.VMEM((2, 9, NBLK, BLK), F32),
            pltpu.VMEM((PAR * NBLK, BLK), F32),
        ],
        compiler_params=pltpu.CompilerParams(vmem_limit_bytes=LIMIT),
        name="finish",
    )(gaussians, passed, inbox, moving_blocks)
    return (rendered, gradients)


def solution(mesh):
    in_specs = (
        P(None, ("groups", "render")),
        P(("groups", "view"), None),
        P(("groups", "view"), None),
        P(("groups", "view"), "render", None, None),
        P(("groups", "view"), "render", None),
        P("groups"),
        P(("groups", "view"), None, "render", None),
    )
    out_specs = (P(("groups", "view"), None, "render", None), P(None, ("groups", "render")))
    return jax.shard_map(shards, mesh=mesh, in_specs=in_specs, out_specs=out_specs, check_vma=False)
```

```python
import functools

import jax
import jax.numpy as jnp
from jax import lax
from jax.experimental import pallas as pl
from jax.experimental.pallas import tpu as pltpu
from jax.sharding import PartitionSpec as P

PAR = 59
BLK = 128
TSIDE = 16
PIX = TSIDE * TSIDE
NBLK = 32
CAP = 2
ROWS = 16
ID_ROW = 9
SENT = 10
CAM_LANE = NBLK
SEG = 8
TOGETHER = 4

LOW_PASS = 0.3
SH_ZERO = 0.28209479177387814
SH_ONE = 0.4886025119029199
SH_TWO = (
    1.0925484305920792,
    -1.0925484305920792,
    0.31539156525252005,
    -1.0925484305920792,
    0.5462742152960396,
)
SH_THREE = (
    -0.5900435899266435,
    2.890611442640554,
    -0.4570457994644658,
    0.3731763325901154,
    -0.4570457994644658,
    1.445305721320277,
    -0.5900435899266435,
)
F32 = jnp.float32
BF16 = jnp.bfloat16
MESH = pl.DeviceIdType.MESH


def harmonics(x, y, z):
    xx, yy, zz = (x * x, y * y, z * z)
    return [
        SH_ZERO * jnp.ones_like(x),
        -SH_ONE * y,
        SH_ONE * z,
        -SH_ONE * x,
        SH_TWO[0] * x * y,
        SH_TWO[1] * y * z,
        SH_TWO[2] * (2.0 * zz - xx - yy),
        SH_TWO[3] * x * z,
        SH_TWO[4] * (xx - yy),
        SH_THREE[0] * y * (3.0 * xx - yy),
        SH_THREE[1] * x * y * z,
        SH_THREE[2] * y * (4.0 * zz - xx - yy),
        SH_THREE[3] * z * (2.0 * zz - 3.0 * xx - 3.0 * yy),
        SH_THREE[4] * x * (4.0 * zz - xx - yy),
        SH_THREE[5] * z * (xx - yy),
        SH_THREE[6] * x * (xx - 3.0 * yy),
    ]


def total_of(terms):
    total = terms[0]
    for term in terms[1:]:
        total = total + term
    return total


def shape_coefs(position, scales, quaternion, cam):
    variance = [jnp.exp(2.0 * s) for s in scales]
    inverse = 1.0 / jnp.sqrt(total_of([c * c for c in quaternion]))
    w, x, y, z = [c * inverse for c in quaternion]
    rotation = [
        [1.0 - 2.0 * (y * y + z * z), 2.0 * (x * y - w * z), 2.0 * (x * z + w * y)],
        [2.0 * (x * y + w * z), 1.0 - 2.0 * (x * x + z * z), 2.0 * (y * z - w * x)],
        [2.0 * (x * z - w * y), 2.0 * (y * z + w * x), 1.0 - 2.0 * (x * x + y * y)],
    ]
    mapped = [
        [total_of([cam[3 * a + i] * rotation[i][k] for i in range(3)]) for k in range(3)]
        for a in range(2)
    ]
    scaled = [mapped[0][k] * variance[k] for k in range(3)]
    cov_xx = total_of([scaled[k] * mapped[0][k] for k in range(3)]) + LOW_PASS
    cov_xy = total_of([scaled[k] * mapped[1][k] for k in range(3)])
    cov_yy = total_of([mapped[1][k] * mapped[1][k] * variance[k] for k in range(3)]) + LOW_PASS
    over = 1.0 / (cov_xx * cov_yy - cov_xy * cov_xy)
    conic_a, conic_b, conic_c = (cov_yy * over, -cov_xy * over, cov_xx * over)
    mean_x = total_of([cam[i] * position[i] for i in range(3)]) + cam[6]
    mean_y = total_of([cam[3 + i] * position[i] for i in range(3)]) + cam[7]
    lin_x = conic_a * mean_x + conic_b * mean_y
    lin_y = conic_b * mean_x + conic_c * mean_y
    const = -0.5 * (lin_x * mean_x + lin_y * mean_y)
    return [-0.5 * conic_a, -0.5 * conic_c, -conic_b, lin_x, lin_y, const]


def basis_of(position, eye):
    direction = [position[i] - eye[i] for i in range(3)]
    inverse = 1.0 / jnp.sqrt(total_of([c * c for c in direction]))
    return harmonics(*[c * inverse for c in direction])


def log_sigmoid(x):
    return jnp.minimum(x, 0.0) - jnp.log1p(jnp.exp(-jnp.abs(x)))


def lane_row(values):
    lane = lax.broadcasted_iota(jnp.int32, (1, BLK), 1)
    row = jnp.zeros((1, BLK), F32)
    for i, value in enumerate(values):
        row = jnp.where(lane == i, value, row)
    return row


def project_all(gauss_ref, cam_ref, eye_ref, rec_ref, par_ref):
    for b in range(NBLK):
        par_ref[pl.ds(b, PAR, stride=NBLK), :] = gauss_ref[:, b * BLK : (b + 1) * BLK].astype(F32)
    cam = [cam_ref[0, i] for i in range(8)]
    eye = [eye_ref[0, i] for i in range(3)]
    cam_row = jnp.broadcast_to(lane_row([0.0] * CAM_LANE + cam + eye), (8, BLK))
    is_id = lax.broadcasted_iota(jnp.int32, (8, BLK), 1) < CAM_LANE

    def chunk(c, carry):
        at = pl.multiple_of(c * 8, 8)

        def par(k):
            return par_ref[pl.ds(k * NBLK + at, 8), :]

        position = [par(k) for k in range(3)]
        coefs = shape_coefs(position, [par(3 + k) for k in range(3)], [par(6 + k) for k in range(4)], cam)
        coefs[5] = coefs[5] + log_sigmoid(par(10))
        basis = basis_of(position, eye)
        rows = []
        for ch in range(3):
            colour = total_of([basis[k] * par(11 + 16 * ch + k) for k in range(16)])
            rows.append(jnp.maximum(colour + 0.5, 0.0))
        rows += coefs
        block_id = (lax.broadcasted_iota(jnp.int32, (8, BLK), 0) + at).astype(F32)
        rows.append(jnp.where(is_id, block_id, cam_row))
        for k in range(ROWS):
            value = rows[k] if k < len(rows) else jnp.zeros((8, BLK), F32)
            rec_ref[pl.ds(at, 8), k, :] = value
        return carry

    lax.fori_loop(0, NBLK // 8, chunk, 0)


def split(values, count):
    pieces = []
    rest = values
    for i in range(count):
        piece = rest.astype(BF16)
        pieces.append(piece)
        if i + 1 < count:
            rest = rest - piece.astype(F32)
    return pieces


def dot_tn(a, b):
    return lax.dot_general(a, b, (((0,), (0,)), ((), ())), preferred_element_type=F32)


def dot_nt(a, b):
    return lax.dot_general(a, b, (((1,), (1,)), ((), ())), preferred_element_type=F32)


def dot_nn(a, b):
    return lax.dot_general(a, b, (((1,), (0,)), ((), ())), preferred_element_type=F32)


def monomials():
    pixel = lax.broadcasted_iota(jnp.int32, (1, PIX), 1)
    middle = (TSIDE - 1) / 2.0
    x = jnp.bitwise_and(pixel, TSIDE - 1).astype(F32) - middle
    y = jnp.right_shift(pixel, 4).astype(F32) - middle
    zero = jnp.zeros_like(x)
    rows = [zero] * 3 + [x * x, y * y, x * y, x, y, zero + 1.0] + [zero] * (ROWS - 9)
    return jnp.concatenate(rows, axis=0).astype(BF16)


def reorder(list_ref, order_ref):
    tiles, entries = list_ref.shape[1:]
    steps = entries // SEG
    for start in range(0, entries, BLK):
        place = lax.broadcasted_iota(jnp.int32, (tiles, BLK), 1) + start
        entry = jnp.bitwise_and(place, SEG - 1) * steps + place // SEG
        lanes = jnp.bitwise_and(entry, BLK - 1)
        found = jnp.zeros((tiles, BLK), jnp.int32)
        for first in range(0, entries, BLK):
            values = list_ref[0, :, first : first + BLK]
            taken = jnp.take_along_axis(values, lanes, axis=1, mode="promise_in_bounds")
            found = jnp.where(entry // BLK == first // BLK, taken, found)
        order_ref[:, start : start + BLK] = found


def render_all(rec_ref, order_ref, cot_ref, image_ref, grad_ref):
    slots = rec_ref.shape[0]
    tiles, entries = order_ref.shape
    group = min(slots, 16)
    grad_ref[...] = jnp.zeros_like(grad_ref)
    mono = monomials()
    mono_three = jnp.concatenate([mono, mono, mono], axis=0)

    def tile(t):
        index = order_ref[pl.ds(t, 1), :]
        lane = jnp.bitwise_and(index, BLK - 1)
        slot = jnp.right_shift(index, 7)
        picked = []
        for start in range(0, entries, BLK):
            lanes = jnp.broadcast_to(lane[:, start : start + BLK], (ROWS, BLK))
            owner = jnp.broadcast_to(slot[:, start : start + BLK], (ROWS, BLK))

            def pick(s, found):
                taken = jnp.take_along_axis(rec_ref[s], lanes, axis=1, mode="promise_in_bounds")
                return jnp.where(owner == s, taken, found)

            found = jnp.zeros((ROWS, BLK), F32)
            if slots <= 16:
                for s in range(slots):
                    found = pick(s, found)
            else:
                found = lax.fori_loop(0, slots, pick, found)
            picked.append(found)
        records = jnp.concatenate(picked, axis=1)
        rec_three = jnp.concatenate(split(records, 3), axis=0)
        cot = [cot_ref[0, ch, pl.ds(t, 1), :] for ch in range(3)] + [jnp.zeros((ROWS - 3, PIX), F32)]
        cot_one, cot_two = split(jnp.concatenate(cot, axis=0), 2)
        power = dot_tn(rec_three, mono_three)
        toward = dot_tn(
            jnp.concatenate([rec_three, rec_three], axis=0),
            jnp.concatenate([cot_one] * 3 + [cot_two] * 3, axis=0),
        )
        steps = entries // SEG
        keep = jnp.ones((SEG, PIX), F32)
        seen = jnp.zeros((SEG, PIX), F32)
        alphas, weights = ([], [])
        for r in range(steps):
            alpha = jnp.exp(power[r * SEG : (r + 1) * SEG])
            weight = alpha * keep
            seen = seen + weight * toward[r * SEG : (r + 1) * SEG]
            keep = keep * (1.0 - alpha)
            alphas.append(alpha)
            weights.append(weight)
        front = [jnp.ones((1, PIX), F32)]
        for s in range(SEG - 1):
            front.append(front[-1] * keep[s : s + 1])
        behind = [jnp.zeros((1, PIX), F32)]
        for s in range(SEG - 1, 0, -1):
            behind.append(seen[s : s + 1] + keep[s : s + 1] * behind[-1])
        front = jnp.concatenate(front, axis=0)
        back = jnp.concatenate(behind[::-1], axis=0)
        slopes = [None] * steps
        for r in range(steps - 1, -1, -1):
            weight = weights[r] * front
            weights[r] = weight
            value = toward[r * SEG : (r + 1) * SEG]
            slopes[r] = weight * (value - back)
            back = alphas[r] * value + (1.0 - alphas[r]) * back
        weight_one, weight_two = split(jnp.concatenate(weights, axis=0), 2)
        slope_one, slope_two = split(jnp.concatenate(slopes, axis=0), 2)
        image = dot_nn(rec_three, weight_one) + dot_nn(rec_three, weight_two)
        image = image[:ROWS] + image[ROWS : 2 * ROWS] + image[2 * ROWS :]
        for ch in range(3):
            image_ref[0, ch, pl.ds(t, 1), :] = image[ch : ch + 1]
        cot_both = jnp.concatenate([cot_one, cot_two], axis=0)
        colour_grad = dot_nt(cot_both, weight_one) + dot_nt(cot_both, weight_two)
        shape_grad = dot_nt(mono, slope_one) + dot_nt(mono, slope_two)
        entry_grad = colour_grad[:ROWS] + colour_grad[ROWS:] + shape_grad
        return split(entry_grad, 2), lane, slot

    together = TOGETHER if tiles % TOGETHER == 0 else 1

    def some_tiles(t, carry):
        drawn = [tile(t * together + i) for i in range(together)]
        pieces = [jnp.concatenate([d[0][i] for d in drawn], axis=1) for i in range(2)]
        lane = jnp.concatenate([d[1] for d in drawn], axis=1)
        slot = jnp.concatenate([d[2] for d in drawn], axis=1)
        here = lax.broadcasted_iota(jnp.int32, (BLK, lane.shape[1]), 0) == lane
        here = here.astype(F32).astype(BF16)

        def spread(first, carry):
            masks = [(slot == first + s).astype(F32).astype(BF16) for s in range(group)]
            parts = [
                dot_nt(jnp.concatenate([piece * mask for mask in masks], axis=0), here)
                for piece in pieces
            ]
            grad_ref[pl.ds(first, group)] += (parts[0] + parts[1]).reshape(group, ROWS, BLK)
            return carry

        if slots == group:
            spread(0, 0)
        else:
            lax.fori_loop(0, slots // group, lambda i, c: spread(i * group, c), 0)
        return carry

    lax.fori_loop(0, tiles // together, some_tiles, 0)
    row = lax.broadcasted_iota(jnp.int32, grad_ref.shape, 1)
    grad_ref[...] = jnp.where(row >= ID_ROW, rec_ref[...], grad_ref[...])


def each(count, body):
    if count <= 16:
        for i in range(count):
            body(i)
    else:
        lax.fori_loop(0, count, lambda i, carry: (body(i), carry)[1], 0)


def scene_kernel(
    owners, gauss_hbm, cam_ref, eye_ref, send_ref, list_hbm, cot_hbm,
    image_ref, back_ref, passed_ref,
    gauss_ref, list_ref, cot_ref, par_ref, rec_ref, out_ref, in_ref, order_ref, grad_ref, ext_ref,
    load_sem, pass_send, pass_recv, rec_send, rec_recv, back_send, back_recv, view_send, view_recv,
):
    me = lax.axis_index("render")
    view = lax.axis_index("view")
    pairs = [(gauss_hbm, gauss_ref), (list_hbm, list_ref), (cot_hbm, cot_ref)]
    loads = [pltpu.make_async_copy(a, b, load_sem.at[i]) for i, (a, b) in enumerate(pairs)]
    for load in loads:
        load.start()
    barrier = pltpu.get_barrier_semaphore()

    def greet(i):
        pl.semaphore_signal(
            barrier, inc=1, device_id={"render": (me + 1 + i) % owners}, device_id_type=MESH
        )

    in_ref[...] = jnp.zeros_like(in_ref)
    each(owners - 1, greet)
    pl.semaphore_signal(barrier, inc=1, device_id={"view": 1 - view}, device_id_type=MESH)
    loads[0].wait()
    project_all(gauss_ref, cam_ref, eye_ref, rec_ref, par_ref)

    def fill(i):
        for c in range(CAP):
            block = jnp.minimum(send_ref[0, 0, i, c], NBLK - 1)
            out_ref[i, c] = rec_ref[block]

    each(owners, fill)
    pl.semaphore_wait(barrier, owners)

    def record_copy(i):
        peer = (me + 1 + i) % owners
        return pltpu.make_async_remote_copy(
            src_ref=out_ref.at[peer, :, pl.ds(0, SENT)], dst_ref=in_ref.at[me, :, pl.ds(0, SENT)],
            send_sem=rec_send.at[i], recv_sem=rec_recv.at[i],
            device_id={"render": peer}, device_id_type=MESH,
        )

    each(owners - 1, lambda i: record_copy(i).start())
    passing = pltpu.make_async_remote_copy(
        src_ref=gauss_hbm, dst_ref=passed_ref, send_sem=pass_send, recv_sem=pass_recv,
        device_id={"render": (me + 1) % owners}, device_id_type=MESH,
    )
    in_ref[me] = out_ref[me]
    loads[1].wait()
    loads[2].wait()
    reorder(list_ref, order_ref)
    each(owners - 1, lambda i: record_copy(i).wait())
    passing.start()
    render_all(in_ref.reshape(owners * CAP, ROWS, BLK), order_ref, cot_ref, image_ref, grad_ref)
    ext_ref[pl.ds(1, owners)] = grad_ref[...].reshape(owners, CAP, ROWS, BLK)
    ext_ref[0] = ext_ref[owners]

    def back_copy(i):
        peer = (me + 1 + i) % owners
        return pltpu.make_async_remote_copy(
            src_ref=ext_ref.at[pl.ds(peer, 2), :, pl.ds(0, SENT)],
            dst_ref=back_ref.at[view, me, :, :, pl.ds(0, SENT)],
            send_sem=back_send.at[i], recv_sem=back_recv.at[i],
            device_id={"render": peer}, device_id_type=MESH,
        )

    def view_copy(i):
        source = (me + owners - i) % owners
        piece = back_ref.at[view, source, :, :, pl.ds(0, SENT)]
        return pltpu.make_async_remote_copy(
            src_ref=piece, dst_ref=piece,
            send_sem=view_send.at[i], recv_sem=view_recv.at[i],
            device_id={"view": 1 - view}, device_id_type=MESH,
        )

    def forward(i):
        back_copy(i).wait_recv()
        view_copy(i + 1).start()

    def settle(i):
        back_copy(i).wait_send()

    each(owners - 1, lambda i: back_copy(i).start())
    back_ref[view, me] = ext_ref[pl.ds(me, 2)]
    view_copy(0).start()
    each(owners - 1, forward)
    each(owners - 1, settle)
    each(owners, lambda i: view_copy(i).wait())
    passing.wait()


def final_kernel(
    own_hbm, prev_hbm, inbox_ref, move_ref, image_hbm, out_ref, image_out,
    own_ref, prev_ref, par_ref, sum_ref, res_ref, load_sem,
):
    pairs = [(own_hbm, own_ref), (prev_hbm, prev_ref), (image_hbm, image_out)]
    loads = [pltpu.make_async_copy(a, b, load_sem.at[i]) for i, (a, b) in enumerate(pairs)]
    for load in loads:
        load.start()
    count = inbox_ref.shape[1] // ROWS
    cams = []
    move_row = lane_row([move_ref[b].astype(F32) for b in range(NBLK)])
    from_prev = jnp.bitwise_and(lax.broadcasted_iota(jnp.int32, (count, BLK), 0) // CAP, 1) == 0
    wanted = from_prev.astype(F32) == move_row
    for v in range(2):
        ids = inbox_ref[v, pl.ds(ID_ROW, count, stride=ROWS), :].astype(jnp.int32)
        hit = (ids == lax.broadcasted_iota(jnp.int32, (count, BLK), 1)) & wanted
        hit = hit.astype(F32).astype(BF16)[:, :NBLK]
        values = jnp.concatenate(
            [inbox_ref[v, pl.ds(k, count, stride=ROWS), :] for k in range(9)], axis=1
        )
        summed = dot_tn(jnp.concatenate([hit] * 3, axis=0), jnp.concatenate(split(values, 3), axis=0))
        for k in range(9):
            sum_ref[v, k] = summed[:, k * BLK : (k + 1) * BLK]
        row = inbox_ref[v, pl.ds(ID_ROW, 1), :]
        cams.append([row[:, CAM_LANE + i : CAM_LANE + i + 1] for i in range(11)])

    loads[0].wait()
    loads[1].wait()
    for b in range(NBLK):
        here = own_ref[:, b * BLK : (b + 1) * BLK].astype(F32)
        there = prev_ref[:, b * BLK : (b + 1) * BLK].astype(F32)
        par_ref[pl.ds(b, PAR, stride=NBLK), :] = jnp.where(move_ref[b] == 1, there, here)

    def chunk(c, carry):
        at = pl.multiple_of(c * 8, 8)

        def par(k):
            return par_ref[pl.ds(k * NBLK + at, 8), :]

        position = [par(k) for k in range(3)]
        scales = [par(3 + k) for k in range(3)]
        quaternion = [par(6 + k) for k in range(4)]
        harmonic_grads = []
        shared = None
        from_const = None
        for v in range(2):
            cam, eye = (cams[v][:8], cams[v][8:])
            grads = [sum_ref[v, k, pl.ds(at, 8), :] for k in range(9)]
            basis, basis_back = jax.vjp(lambda p: basis_of(p, eye), position)
            live = []
            for ch in range(3):
                colour = total_of([basis[k] * par(11 + 16 * ch + k) for k in range(16)]) + 0.5
                live.append(grads[ch] * jnp.where(colour > 0.0, 1.0, jnp.where(colour == 0.0, 0.5, 0.0)))
            for ch in range(3):
                for k in range(16):
                    slope = basis[k] * live[ch]
                    if v == 0:
                        harmonic_grads.append(slope)
                    else:
                        res_ref[pl.ds((11 + 16 * ch + k) * NBLK + at, 8), :] = (
                            harmonic_grads[16 * ch + k] + slope
                        )
            basis_cot = [
                total_of([live[ch] * par(11 + 16 * ch + k) for ch in range(3)]) for k in range(16)
            ]
            moved = basis_back(basis_cot)[0]
            _, shape_back = jax.vjp(
                lambda p, s, q: shape_coefs(p, s, q, cam), position, scales, quaternion
            )
            p_grad, s_grad, q_grad = shape_back(grads[3:9])
            p_grad = [p_grad[i] + moved[i] for i in range(3)]
            every = p_grad + list(s_grad) + list(q_grad)
            shared = every if v == 0 else [shared[i] + every[i] for i in range(10)]
            from_const = grads[8] if v == 0 else from_const + grads[8]
        shared.append(from_const * jax.nn.sigmoid(-par(10)))
        for k in range(11):
            res_ref[pl.ds(k * NBLK + at, 8), :] = shared[k]
        return carry

    lax.fori_loop(0, NBLK // 8, chunk, 0)
    for b in range(NBLK):
        out_ref[:, b * BLK : (b + 1) * BLK] = res_ref[pl.ds(b, PAR, stride=NBLK), :]
    loads[2].wait()


VMEM = pl.BlockSpec(memory_space=pltpu.VMEM)
ANY = pl.BlockSpec(memory_space=pl.ANY)
SMEM = pl.BlockSpec(memory_space=pltpu.SMEM)
LIMIT = 63 * 1024 * 1024


def shards(gaussians, camera, eye_point, send_lists, tile_lists, moving_blocks, image_grad):
    owners = lax.axis_size("render")
    views = lax.axis_size("view")
    slots = owners * CAP
    tiles, entries = tile_lists.shape[1:]
    dma = pltpu.SemaphoreType.DMA
    rendered, back, passed = pl.pallas_call(
        functools.partial(scene_kernel, owners),
        out_shape=[
            jax.ShapeDtypeStruct(image_grad.shape, F32),
            jax.ShapeDtypeStruct((views, owners, 2, CAP, ROWS, BLK), F32),
            jax.ShapeDtypeStruct(gaussians.shape, BF16),
        ],
        in_specs=[ANY, SMEM, SMEM, SMEM, ANY, ANY],
        out_specs=[VMEM, VMEM, ANY],
        scratch_shapes=[
            pltpu.VMEM(gaussians.shape, BF16),
            pltpu.VMEM(tile_lists.shape, jnp.int32),
            pltpu.VMEM(image_grad.shape, F32),
            pltpu.VMEM((PAR * NBLK, BLK), F32),
            pltpu.VMEM((NBLK, ROWS, BLK), F32),
            pltpu.VMEM((owners, CAP, ROWS, BLK), F32),
            pltpu.VMEM((owners, CAP, ROWS, BLK), F32),
            pltpu.VMEM((tiles, entries), jnp.int32),
            pltpu.VMEM((slots, ROWS, BLK), F32),
            pltpu.VMEM((owners + 1, CAP, ROWS, BLK), F32),
            dma((3,)), dma, dma,
            dma((owners - 1,)), dma((owners - 1,)),
            dma((owners - 1,)), dma((owners - 1,)),
            dma((owners,)), dma((owners,)),
        ],
        compiler_params=pltpu.CompilerParams(
            vmem_limit_bytes=LIMIT, collective_id=0, has_side_effects=True
        ),
        name="scene",
    )(gaussians, camera, eye_point, send_lists, tile_lists, image_grad)
    inbox = back.reshape(views, owners * 2 * CAP * ROWS, BLK)
    gradients, image = pl.pallas_call(
        final_kernel,
        out_shape=[
            jax.ShapeDtypeStruct(gaussians.shape, F32),
            jax.ShapeDtypeStruct(rendered.shape, F32),
        ],
        in_specs=[ANY, ANY, VMEM, SMEM, ANY],
        out_specs=[VMEM, ANY],
        scratch_shapes=[
            pltpu.VMEM(gaussians.shape, BF16),
            pltpu.VMEM(gaussians.shape, BF16),
            pltpu.VMEM((PAR * NBLK, BLK), F32),
            pltpu.VMEM((2, 9, NBLK, BLK), F32),
            pltpu.VMEM((PAR * NBLK, BLK), F32),
            dma((3,)),
        ],
        compiler_params=pltpu.CompilerParams(vmem_limit_bytes=LIMIT),
        name="finish",
    )(gaussians, passed, inbox, moving_blocks, rendered)
    return (image, gradients)


def solution(mesh):
    in_specs = (
        P(None, ("groups", "render")),
        P(("groups", "view"), None),
        P(("groups", "view"), None),
        P(("groups", "view"), "render", None, None),
        P(("groups", "view"), "render", None),
        P("groups"),
        P(("groups", "view"), None, "render", None),
    )
    out_specs = (P(("groups", "view"), None, "render", None), P(None, ("groups", "render")))
    return jax.shard_map(shards, mesh=mesh, in_specs=in_specs, out_specs=out_specs, check_vma=False)
```
